32 devices in a mesh: ctx: 4 (over x, core), shard: 8 (over z, y).
Axes of the slice: x: 2, y: 2, z: 4, core: 2. Of those that a mesh axis runs over, the one named last changes fastest.
Arguments:
- layer_input: bfloat16 [16, 1024, 1536], P('shard', 'ctx'), may hold values from -6 to 6
- cotangent: bfloat16 [16, 1024, 1536], P('shard', 'ctx'), may hold values from -6 to 6
- seq_lengths: int32 [16], P('shard'), may hold values from 256 to 1024, as said below
- routes: int32 [16, 1024, 4], P('shard', 'ctx'), may hold values from 0 to 15, all different within a row
- drop_order: int32 [16, 1024], P('shard', 'ctx'), may hold values from 0 to 1023, each once within a row
- block_order: int32 [8], replicated, may hold values from 0 to 7, each once
- attn_gain: bfloat16 [1536], P('shard'), may hold values from 0.5 to 1.5
- query_weight: bfloat16 [1536, 1536], P('shard'), may hold values from -0.15625 to 0.15625
- keyval_weight: bfloat16 [1536, 512], P('shard'), may hold values from -0.15625 to 0.15625
- output_weight: bfloat16 [1536, 1536], P('shard'), may hold values from -0.625 to 0.625
- moe_gain: bfloat16 [1536], P('shard'), may hold values from 0.5 to 1.5
- router_weight: bfloat16 [1536, 16], P('shard'), may hold values from -0.078125 to 0.078125
- expert_in: bfloat16 [16, 1536, 1536], P('shard', 'ctx'), may hold values from -0.15625 to 0.15625
- expert_out: bfloat16 [16, 768, 1536], P('shard', 'ctx'), may hold values from -0.21875 to 0.21875
Outputs:
- output: bfloat16 [16, 1024, 1536], P('shard', 'ctx')
- grad_input: bfloat16 [16, 1024, 1536], P('shard', 'ctx')
- grad_attn_gain: float32 [1536], P('shard')
- grad_query_weight: float32 [1536, 1536], P('shard')
- grad_keyval_weight: float32 [1536, 512], P('shard')
- grad_output_weight: float32 [1536, 1536], P('shard')
- grad_moe_gain: float32 [1536], P('shard')
- grad_router_weight: float32 [1536, 16], P('shard')
- grad_expert_in: float32 [16, 1536, 1536], P('shard', 'ctx')
- grad_expert_out: float32 [16, 768, 1536], P('shard', 'ctx')
The draws below stay inside these ranges and needn't reach their ends.
Inputs may be any that keep to these rules, and one draw needn't show every extreme that they name: `seq_lengths`: among the 2 sequences of each index of shard one has length 1024. `routes`: each token names 4 different experts. `drop_order`: each sequence's row is a permutation. `block_order`: a permutation.
All inputs are finite; a program needn't handle non-finite values.
Results may differ from the reference program's by a relative error of at most 0.022.
Values may be sent and summed in bfloat16 or wider, within the bound.
No kernel may reach another device: no remote copies, remote signals or barrier semaphores. Data moves between devices by JAX's collectives and lax.ppermute only.
A program may use at most 256 MiB of HBM per device.

```python
import jax
import jax.numpy as jnp
from jax import lax

D = 1536
H = 12
KVH = 2
HD = 128
FF = 768
TOPK = 4
SEQ_SH = 2
BLK = 256
L = 1024
SEQS = 16
EXPERTS = 16
CAP = 160
N_CTX = 4
N_SHARD = 8


def draw_seq_lengths(key, part):
    key = jax.random.fold_in(key, 11)
    length_key, pick_key = jax.random.split(key)
    drawn_lengths = jax.random.randint(length_key, (SEQS,), L // 4, L + 1)
    groups = SEQS // SEQ_SH
    longest = jax.random.randint(pick_key, (groups,), 0, SEQ_SH)
    chosen = jnp.arange(SEQS) % SEQ_SH == jnp.repeat(longest, SEQ_SH, total_repeat_length=SEQS)
    return jnp.where(chosen, L, drawn_lengths).astype(jnp.int32)


def block_scale(own_key, shape, pieces, least, largest):
    loudness, own = 1.0, jax.random.fold_in(own_key, 6)
    for position, parts in pieces:
        steps = jnp.exp(jax.random.uniform(jax.random.fold_in(own, position), (parts,), jnp.float32, least / len(pieces), largest / len(pieces)))
        loudness = loudness * jnp.repeat(steps, shape[position] // parts).reshape([-1 if axis == position else 1 for axis in range(len(shape))])
    return loudness


def different_ones(rng, rows, amount, top, lift):
    order = jax.random.permutation(jax.random.fold_in(rng, 1), amount)
    boost = order
    for power in range(3):
        boost = boost * boost // amount
    boost = boost * lift // amount
    chance = jax.random.randint(jax.random.fold_in(rng, 2), (rows, amount), 0, 4096) + boost
    fixed_rows = jax.random.permutation(jax.random.fold_in(rng, 3), rows)[jnp.arange(amount) % rows]
    chance = jnp.where(jnp.arange(rows)[:, None] == fixed_rows[None, :], 1 << 14, chance)
    score = chance * amount + jnp.arange(amount)
    return lax.top_k(score.astype(jnp.int32), top)[1].astype(jnp.int32)


def centred(stream_key, shape, scale, bound, cuts=(), held_as=jnp.bfloat16):
    loudness = block_scale(stream_key, shape, cuts, -0.22, 0.18) if cuts else 1.0
    values = jax.random.normal(stream_key, shape, jnp.float32) * scale * loudness
    return jnp.minimum(jnp.maximum(values, -bound), bound).astype(held_as)


def setup_inputs(seed: int = 0) -> dict:
    key_list = jax.random.split(jax.random.key(seed), 15)
    layer_input = centred(key_list[0], (SEQS, L, D), 1.0, 6.0, ((0, 8), (1, 4)))
    cotangent = centred(key_list[1], (SEQS, L, D), 1.0, 6.0, ((0, 8), (1, 4)))
    seq_lengths = draw_seq_lengths(jax.random.fold_in(key_list[14], 71), 0)
    routes = different_ones(key_list[3], SEQS * L, EXPERTS, TOPK, 2048).reshape((SEQS, L, TOPK))
    drop_order = jax.vmap(lambda own: jax.random.permutation(own, L))(jax.random.split(key_list[4], SEQS)).reshape((SEQS, L)).astype(jnp.int32)
    block_order = jax.random.permutation(key_list[5], 2 * N_CTX).astype(jnp.int32)
    attn_gain = jnp.clip(1.0 + 0.1 * jax.random.normal(key_list[6], (D,), jnp.float32), 0.5, 1.5).astype(jnp.bfloat16)
    query_weight = centred(key_list[7], (D, H * HD), D ** -0.5, 0.15625, ((0, 8),))
    keyval_weight = centred(key_list[8], (D, 2 * KVH * HD), D ** -0.5, 0.15625, ((0, 8),))
    output_weight = centred(key_list[9], (H * HD, D), (H * HD // 16) ** -0.5, 0.625, ((0, 8),))
    moe_gain = jnp.clip(1.0 + 0.1 * jax.random.normal(key_list[10], (D,), jnp.float32), 0.5, 1.5).astype(jnp.bfloat16)
    router_weight = centred(key_list[11], (D, EXPERTS), (4 * D) ** -0.5, 0.078125, ((0, 8),))
    expert_in = centred(key_list[12], (EXPERTS, D, 2 * FF), D ** -0.5, 0.15625, ((0, 8), (1, 4)))
    expert_out = centred(key_list[13], (EXPERTS, FF, D), FF ** -0.5, 0.21875, ((0, 8), (1, 4)))
    return {"layer_input": layer_input, "cotangent": cotangent, "seq_lengths": seq_lengths, "routes": routes, "drop_order": drop_order, "block_order": block_order, "attn_gain": attn_gain, "query_weight": query_weight, "keyval_weight": keyval_weight, "output_weight": output_weight, "moe_gain": moe_gain, "router_weight": router_weight, "expert_in": expert_in, "expert_out": expert_out}


EPSILON = 1e-06
ROPE_BASE = 10000.0
HIGHEST = lax.Precision.HIGHEST
NEG_FILL = -1e+30

@jax.custom_vjp
def low(v):
    return lax.optimization_barrier(v.astype(jnp.bfloat16)).astype(jnp.float32)

@jax.custom_vjp
def low_back(v):
    return v

def low_keep(v):
    return (low(v), None)

def low_pass(kept, grad):
    return (grad,)

def back_keep(v):
    return (v, None)

def back_low(kept, grad):
    return (low(grad),)
low.defvjp(low_keep, low_pass)
low_back.defvjp(back_keep, back_low)

def rms_norm(values, gain):
    return values * lax.rsqrt(lax.optimization_barrier(jnp.mean(values * values, axis=-1, keepdims=True)) + EPSILON) * gain

def positions_of(block_order, length):
    sub_len = length // block_order.shape[0]
    storage = jnp.arange(length, dtype=jnp.int32)
    return block_order[storage // sub_len] * sub_len + storage % sub_len

def rope_tables(positions, width):
    half_width = width // 2
    frequency = ROPE_BASE ** (-2.0 * jnp.arange(half_width, dtype=jnp.float32) / width)
    angles = positions.astype(jnp.float32)[:, None] * frequency[None, :]
    return (jnp.cos(angles), jnp.sin(angles))

def rotate(values, cosine_table, sine_table):
    half_width = values.shape[-1] // 2
    first_half = values[..., :half_width]
    second_half = values[..., half_width:]
    cosine_part = cosine_table[:, None, :]
    sine_part = sine_table[:, None, :]
    return jnp.concatenate([first_half * cosine_part - second_half * sine_part, second_half * cosine_part + first_half * sine_part], axis=-1)

def attend(query_seq, key_seq, value_seq, positions, length):
    seq_len = query_seq.shape[0]
    block_rows = min(512, seq_len)
    group_ratio = H // KVH
    scale = HD ** (-0.5)

    def block_step(block_num):
        query_block = lax.dynamic_slice_in_dim(query_seq, block_num * block_rows, block_rows, 0).reshape(block_rows, KVH, group_ratio, HD)
        query_pos = lax.dynamic_slice_in_dim(positions, block_num * block_rows, block_rows, 0)
        scores = jnp.einsum('qgrd,kgd->gqrk', query_block, key_seq, precision=HIGHEST) * scale
        scores = low_back(scores)
        allowed = (positions[None, :] <= query_pos[:, None]) & (positions[None, :] < length)
        allowed = allowed[None, :, None, :]
        masked = jnp.where(allowed, scores, NEG_FILL)
        row_max = lax.optimization_barrier(jnp.max(masked, axis=-1, keepdims=True))
        weights = jnp.where(allowed, jnp.exp(masked - row_max), 0.0)
        probs = low(weights / lax.optimization_barrier(jnp.sum(weights, axis=-1, keepdims=True)))
        result = jnp.einsum('gqrk,kgd->qgrd', probs, value_seq, precision=HIGHEST)
        return result.reshape(block_rows, H * HD)
    blocks = lax.map(jax.checkpoint(block_step), jnp.arange(seq_len // block_rows))
    return blocks.reshape(seq_len, H * HD)

def to_devices(values):
    rest = values.shape[2:]
    values = values.reshape((N_SHARD, SEQ_SH, N_CTX, BLK) + rest)
    values = jnp.moveaxis(values, 2, 0)
    return values.reshape((N_CTX, N_SHARD, SEQ_SH * BLK) + rest)

def from_devices(values):
    rest = values.shape[3:]
    values = values.reshape((N_CTX, N_SHARD, SEQ_SH, BLK) + rest)
    values = jnp.moveaxis(values, 0, 2)
    return values.reshape((SEQS, N_CTX * BLK) + rest)

def take_rows(matrix_rows, row_numbers):
    return matrix_rows[row_numbers]

def route_tables(token_routes, token_order, token_live, token_seq):
    token_count = token_routes.shape[0]
    every_expert = jnp.arange(EXPERTS, dtype=jnp.int32)
    route_hit = (token_routes[:, :, None] == every_expert[None, None, :]) & token_live[:, None, None]
    expert_load = lax.optimization_barrier(jnp.sum(route_hit.astype(jnp.int32), axis=1)).astype(jnp.int32)
    priority = (token_order * SEQ_SH + token_seq).astype(jnp.int32)
    ranking = jnp.argsort(priority, stable=True).astype(jnp.int32)
    sorted_load = expert_load[ranking]
    ahead_sorted = (jnp.cumsum(sorted_load, axis=0) - sorted_load).astype(jnp.int32)
    ahead_count = jnp.zeros((token_count, EXPERTS), jnp.int32).at[ranking].set(ahead_sorted)
    slot_of = jnp.take_along_axis(ahead_count, token_routes, axis=1).astype(jnp.int32)
    is_kept = token_live[:, None] & (slot_of < CAP)
    target = jnp.where(is_kept, token_routes * CAP + slot_of, 0).reshape(-1).astype(jnp.int32)
    slot_target = jnp.where(is_kept, token_routes * CAP + slot_of, EXPERTS * CAP).reshape(-1).astype(jnp.int32)
    source = jnp.full((EXPERTS * CAP + 1,), token_count * TOPK, jnp.int32)
    source = source.at[slot_target].set(jnp.arange(token_count * TOPK, dtype=jnp.int32))
    return (is_kept, target, source[:EXPERTS * CAP])

def forward(layer_input, attn_gain, query_weight, keyval_weight, output_weight, moe_gain, router_weight, expert_in, expert_out, context):
    cosine_table, sine_table, positions, seq_lengths, device_routes, kept_float, target, source = context
    hidden = low(rms_norm(layer_input, attn_gain))
    query_raw = low_back(jnp.dot(hidden, query_weight, precision=HIGHEST))
    keyval_raw = low_back(jnp.dot(hidden, keyval_weight, precision=HIGHEST))
    queries = low(rotate(query_raw.reshape(SEQS, L, H, HD), cosine_table, sine_table))
    keyval_raw = keyval_raw.reshape(SEQS, L, 2, KVH, HD)
    keys = low(rotate(keyval_raw[:, :, 0], cosine_table, sine_table))
    values = low(keyval_raw[:, :, 1])
    attended = lax.map(lambda item: attend(item[0], item[1], item[2], positions, item[3]), (queries, keys, values, seq_lengths))
    attended = low_back(low(attended))
    branch = low_back(jnp.dot(attended, output_weight, precision=HIGHEST))
    middle = layer_input + branch
    tokens = to_devices(low(rms_norm(middle, moe_gain)))
    logits = jnp.dot(tokens, router_weight, precision=HIGHEST)
    chosen = jnp.take_along_axis(logits, device_routes, axis=-1)
    gates = jax.nn.softmax(chosen, axis=-1) * kept_float
    padded = jnp.concatenate([tokens, jnp.zeros((N_CTX, N_SHARD, 1, D), tokens.dtype)], axis=2)
    dispatched = jax.vmap(jax.vmap(take_rows))(padded, source // TOPK)
    dispatched = low_back(dispatched).reshape(N_CTX, N_SHARD, EXPERTS, CAP, D)

    def expert_step(expert_num):
        expert_rows = dispatched[:, :, expert_num]
        both = low_back(jnp.einsum('csqd,df->csqf', expert_rows, expert_in[expert_num], precision=HIGHEST))
        active = low(jax.nn.silu(both[..., :FF]) * both[..., FF:])
        return low_back(low(jnp.einsum('csqf,fd->csqd', active, expert_out[expert_num], precision=HIGHEST)))
    results = lax.map(jax.checkpoint(expert_step), jnp.arange(EXPERTS))
    results = jnp.moveaxis(results, 0, 2).reshape(N_CTX, N_SHARD, EXPERTS * CAP, D)
    picked = jax.vmap(jax.vmap(take_rows))(results, target).reshape(N_CTX, N_SHARD, SEQ_SH * BLK, TOPK, D)
    mixture = lax.optimization_barrier(jnp.sum(gates[..., None] * picked, axis=3))
    return middle + from_devices(mixture)

def reference(layer_input, cotangent, seq_lengths, routes, drop_order, block_order, attn_gain, query_weight, keyval_weight, output_weight, moe_gain, router_weight, expert_in, expert_out):
    positions = positions_of(block_order, L)
    live = positions[None, :] < seq_lengths[:, None]
    cosine_table, sine_table = rope_tables(positions, HD)
    local_seq = jnp.broadcast_to((jnp.arange(SEQS, dtype=jnp.int32) % SEQ_SH)[:, None], (SEQS, L))
    device_routes = to_devices(routes)
    is_kept, target, source = jax.vmap(jax.vmap(route_tables))(device_routes, to_devices(drop_order), to_devices(live), to_devices(local_seq))
    context = (cosine_table, sine_table, positions, seq_lengths, device_routes, is_kept.astype(jnp.float32), target, source)
    params = tuple((item.astype(jnp.float32) for item in (layer_input, attn_gain, query_weight, keyval_weight, output_weight, moe_gain, router_weight, expert_in, expert_out)))

    def run(*weights):
        return forward(*weights, context)
    result, pull = jax.vjp(run, *params)
    grads = pull(cotangent.astype(jnp.float32) * live[..., None].astype(jnp.float32))
    return (result.astype(jnp.bfloat16), grads[0].astype(jnp.bfloat16), grads[1], grads[2], grads[3], grads[4], grads[5], grads[6], grads[7], grads[8])
```

```python
import functools

import jax
import jax.numpy as jnp
from jax import lax
from jax.experimental import pallas as pl
from jax.experimental.pallas import tpu as pltpu
from jax.sharding import Mesh
from jax.sharding import PartitionSpec as P

H = 12
KVH = 2
HD = 128
FF = 768
TOPK = 4
GROUP = H // KVH

EPSILON = 1e-06
ROPE_BASE = 10000.0
HIGHEST = lax.Precision.HIGHEST
NEG_FILL = -1e30
LOG2E = 1.4426950408889634
SCALE = HD ** (-0.5)
VMEM_LIMIT = 60 * 1024 * 1024
F32 = jnp.float32
BF16 = jnp.bfloat16


def params(limit=VMEM_LIMIT):
    return pltpu.CompilerParams(vmem_limit_bytes=limit)


def nt(a, b, precision=None):
    return lax.dot_general(
        a, b, (((1,), (1,)), ((), ())), precision=precision, preferred_element_type=F32
    )


def tn(a, b, precision=None):
    return lax.dot_general(
        a, b, (((0,), (0,)), ((), ())), precision=precision, preferred_element_type=F32
    )


def nn(a, b, precision=None):
    return jnp.dot(a, b, precision=precision, preferred_element_type=F32)


def swap(value, axis, bit=1):
    size = lax.axis_size(axis)
    return lax.ppermute(value, axis, [(i, i ^ bit) for i in range(size)])


def bits_of(axis):
    size = lax.axis_size(axis)
    return [1 << k for k in range(size.bit_length() - 1)]


def add_low(a, b):
    return (a.astype(F32) + b.astype(F32)).astype(BF16)


def pick(value, index, axis):
    return lax.dynamic_index_in_dim(value, index, axis, keepdims=False)


def gather_group(part, low_first):
    bits = bits_of("l")
    count = len(bits)
    value = part.reshape((1,) * count + part.shape)
    order = range(count) if low_first else reversed(range(count))
    for k in order:
        value = jnp.concatenate([value, swap(value, "l", bits[k])], axis=count - 1 - k)
    return value.reshape((1 << count,) + part.shape)


def reduce_group(value, low_first):
    bits = bits_of("l")
    count = len(bits)
    order = list(range(count) if low_first else reversed(range(count)))
    rest = value.shape[1:]
    value = value.reshape((2,) * count + rest)
    for k in order:
        axis = count - 1 - k
        keep = lax.slice_in_dim(value, 0, 1, axis=axis)
        send = lax.slice_in_dim(value, 1, 2, axis=axis)
        value = add_low(keep, swap(send, "l", bits[k]))
    return value.reshape(rest)


def gather_expert(weight):
    local, rows, columns = weight.shape
    half = local // 2
    core, high = lax.axis_index("c"), lax.axis_index("h")
    keep = lax.dynamic_slice_in_dim(weight, core * half, half, 0)
    send = lax.dynamic_slice_in_dim(weight, (1 - core) * half, half, 0)
    other = swap(send, "c")
    pair = jnp.where(
        core == 0, jnp.stack([keep, other], axis=1), jnp.stack([other, keep], axis=1)
    )
    pieces = [jnp.stack([pair])]
    far = swap(pair, "t")
    n_high = lax.axis_size("h")
    whole = jnp.zeros((2, half, n_high, 2, rows, columns), weight.dtype)
    for t, piece in enumerate((pair, far)):
        pieces = [piece]
        for bit in bits_of("h"):
            pieces = pieces + [swap(p, "h", bit) for p in pieces]
        for r, p in enumerate(pieces):
            whole = lax.dynamic_update_slice(
                whole, p[None, :, None], (t, 0, high ^ r, 0, 0, 0)
            )
    return whole.reshape(2 * half, n_high * 2 * rows, columns)


def reduce_expert(grad, local):
    half = local // 2
    core, high = lax.axis_index("c"), lax.axis_index("h")
    n_high = lax.axis_size("h")
    rows = grad.shape[1] // (2 * n_high)
    value = grad.reshape(2, half, n_high, 2, rows, grad.shape[2])
    width = n_high
    for bit in reversed(bits_of("h")):
        width //= 2
        side = (high & bit) // bit
        keep = lax.dynamic_slice_in_dim(value, side * width, width, 2)
        send = lax.dynamic_slice_in_dim(value, (1 - side) * width, width, 2)
        value = add_low(keep, swap(send, "h", bit))
    value = value.reshape(2, half, 2, rows, grad.shape[2])
    value = add_low(value[0], swap(value[1], "t"))
    keep = pick(value, core, 1)
    other = swap(pick(value, 1 - core, 1), "c")
    return jnp.where(
        core == 0, jnp.concatenate([keep, other]), jnp.concatenate([other, keep])
    ).astype(F32)


def reduce_weight(grad):
    core = lax.axis_index("c")
    low, top = lax.axis_index("l"), lax.axis_index("t")
    n_low = lax.axis_size("l")
    rows, columns = grad.shape[0] // (4 * n_low), grad.shape[1]
    value = grad.reshape(2, n_low, 2, rows, columns)
    value = add_low(pick(value, core, 2), swap(pick(value, 1 - core, 2), "c"))
    count = n_low
    for bit in bits_of("l"):
        count //= 2
        value = value.reshape(2, count, 2, rows, columns)
        side = (low & bit) // bit
        value = add_low(pick(value, side, 2), swap(pick(value, 1 - side, 2), "l", bit))
    value = value.reshape(2, rows, columns)
    value = add_low(pick(value, top, 0), swap(pick(value, 1 - top, 0), "t"))
    for bit in bits_of("h"):
        value = add_low(value, swap(value, "h", bit))
    other = swap(value, "c")
    return jnp.where(
        core == 0, jnp.concatenate([value, other]), jnp.concatenate([other, value])
    ).astype(F32)


def norm_back(grad_normed, gain, normed, inverse):
    scaled = grad_normed * gain
    return inverse * (scaled - normed * jnp.mean(scaled * normed, axis=-1, keepdims=True))


def turn(values, cosine, sine):
    return values * cosine + pltpu.roll(values, HD // 2, 1) * sine


def project_kernel(x_ref, gain_ref, w_ref, cos_ref, sin_ref, hidden_ref, out_ref):
    step = pl.program_id(0)

    @pl.when(step == 0)
    def _():
        x = x_ref[...].astype(F32)
        inverse = lax.rsqrt(jnp.mean(x * x, axis=-1, keepdims=True) + EPSILON)
        hidden_ref[...] = ((x * inverse) * gain_ref[...]).astype(BF16)

    raw = nn(hidden_ref[...], w_ref[...])
    per_step = raw.shape[1] // HD
    for k in range(per_step):
        head = raw[:, k * HD : (k + 1) * HD]
        turned = turn(head, cos_ref[...], sin_ref[...])
        is_value = step * per_step + k >= H + KVH
        out_ref[:, k * HD : (k + 1) * HD] = jnp.where(is_value, head, turned).astype(BF16)


def project(x, gain, weight, cosine, sine):
    rows, width = x.shape
    columns = weight.shape[1]
    block = 512
    return pl.pallas_call(
        project_kernel,
        grid=(columns // block,),
        in_specs=[
            pl.BlockSpec((rows, width), lambda i: (0, 0)),
            pl.BlockSpec((1, width), lambda i: (0, 0)),
            pl.BlockSpec((width, block), lambda i: (0, i)),
            pl.BlockSpec((rows, HD), lambda i: (0, 0)),
            pl.BlockSpec((rows, HD), lambda i: (0, 0)),
        ],
        out_specs=[
            pl.BlockSpec((rows, width), lambda i: (0, 0)),
            pl.BlockSpec((rows, block), lambda i: (0, i)),
        ],
        out_shape=[
            jax.ShapeDtypeStruct((rows, width), BF16),
            jax.ShapeDtypeStruct((rows, columns), BF16),
        ],
        compiler_params=params(),
        cost_estimate=pl.CostEstimate(
            flops=2 * rows * width * columns,
            bytes_accessed=2 * (2 * rows * width + width * columns + rows * columns),
            transcendentals=0,
        ),
        name="project",
    )(x, gain, weight, cosine, sine)


def set_bias(len_ref, posk_ref, posq_ref, bias):
    seq = pl.program_id(0)

    @pl.when((pl.program_id(1) == 0) & (pl.program_id(2) == 0))
    def _():
        posk = posk_ref[...]
        allowed = (posk <= posq_ref[...]) & (posk < len_ref[seq])
        bias[...] = jnp.where(allowed, 0.0, NEG_FILL)


def attend_kernel(len_ref, q_ref, k_ref, v_ref, posk_ref, posq_ref, out_ref, lse_ref, bias, turned):
    set_bias(len_ref, posk_ref, posq_ref, bias)

    @pl.when(pl.program_id(2) == 0)
    def _():
        turned[...] = v_ref[0].T

    scores = nt(k_ref[0], q_ref[...]) * (SCALE * LOG2E) + bias[...]
    top = jnp.max(scores, axis=0, keepdims=True)
    weights = jnp.exp2(scores - top)
    total = jnp.sum(weights, axis=0, keepdims=True)
    mixed = nn(turned[...], weights.astype(BF16)) * (1.0 / total)
    out_ref[...] = mixed.T.astype(BF16)
    lse_ref[0, 0] = top + jnp.log2(total)


def attend(lengths, qkv, keyval, posk, posq):
    seqs, keys, _ = keyval.shape
    rows = qkv.shape[0] // seqs
    return pl.pallas_call(
        attend_kernel,
        grid_spec=pltpu.PrefetchScalarGridSpec(
            num_scalar_prefetch=1,
            grid=(seqs, KVH, GROUP),
            in_specs=[
                pl.BlockSpec((rows, HD), lambda s, g, h, n: (s, g * GROUP + h)),
                pl.BlockSpec((1, keys, HD), lambda s, g, h, n: (s, 0, g)),
                pl.BlockSpec((1, keys, HD), lambda s, g, h, n: (s, 0, KVH + g)),
                pl.BlockSpec((keys, 1), lambda s, g, h, n: (0, 0)),
                pl.BlockSpec((1, rows), lambda s, g, h, n: (0, 0)),
            ],
            out_specs=[
                pl.BlockSpec((rows, HD), lambda s, g, h, n: (s, g * GROUP + h)),
                pl.BlockSpec((1, 1, 1, rows), lambda s, g, h, n: (s, g * GROUP + h, 0, 0)),
            ],
            scratch_shapes=[pltpu.VMEM((keys, rows), F32), pltpu.VMEM((HD, keys), BF16)],
        ),
        out_shape=[
            jax.ShapeDtypeStruct((seqs * rows, H * HD), BF16),
            jax.ShapeDtypeStruct((seqs, H, 1, rows), F32),
        ],
        compiler_params=params(),
        cost_estimate=pl.CostEstimate(
            flops=4 * seqs * H * rows * keys * HD,
            bytes_accessed=4 * seqs * (rows * H * HD + keys * 2 * KVH * HD),
            transcendentals=seqs * H * rows * keys,
        ),
        name="attend",
    )(lengths, qkv, keyval, keyval, posk, posq)


def attend_back_kernel(
    len_ref, q_ref, k_ref, v_ref, posk_ref, posq_ref, grad_ref, out_ref, lse_ref, cos_ref, sin_ref,
    dq_ref, dkv_ref, bias, turned, dk, dv,
):
    set_bias(len_ref, posk_ref, posq_ref, bias)
    head = pl.program_id(2)

    @pl.when(head == 0)
    def _():
        turned[...] = k_ref[0].T
        dk[...] = jnp.zeros_like(dk)
        dv[...] = jnp.zeros_like(dv)

    q, grad = q_ref[...], grad_ref[...]
    scores = nt(k_ref[0], q) * (SCALE * LOG2E) + bias[...]
    probs = jnp.exp2(scores - lse_ref[0, 0])
    grad_probs = nt(v_ref[0], grad)
    product = grad.astype(F32) * out_ref[...].astype(F32)
    delta = jnp.sum(product.T, axis=0, keepdims=True)
    grad_scores = (probs * (grad_probs - delta)).astype(BF16)
    dv[...] += nn(probs.astype(BF16), grad)
    dk[...] += nn(grad_scores, q)
    dq = nn(turned[...], grad_scores).T * SCALE
    dq_ref[...] = turn(dq, cos_ref[...], -sin_ref[...]).astype(BF16)

    @pl.when(head == GROUP - 1)
    def _():
        dkv_ref[0, 0] = (dk[...] * SCALE).astype(BF16)
        dkv_ref[1, 0] = dv[...].astype(BF16)


def attend_back(lengths, qkv, keyval, posk, posq, grad, attended, lse, cosine, sine):
    seqs, keys, _ = keyval.shape
    rows = qkv.shape[0] // seqs
    heads = pl.BlockSpec((rows, HD), lambda s, g, h, n: (s, g * GROUP + h))
    table = pl.BlockSpec((rows, HD), lambda s, g, h, n: (0, 0))
    return pl.pallas_call(
        attend_back_kernel,
        grid_spec=pltpu.PrefetchScalarGridSpec(
            num_scalar_prefetch=1,
            grid=(seqs, KVH, GROUP),
            in_specs=[
                heads,
                pl.BlockSpec((1, keys, HD), lambda s, g, h, n: (s, 0, g)),
                pl.BlockSpec((1, keys, HD), lambda s, g, h, n: (s, 0, KVH + g)),
                pl.BlockSpec((keys, 1), lambda s, g, h, n: (0, 0)),
                pl.BlockSpec((1, rows), lambda s, g, h, n: (0, 0)),
                heads,
                heads,
                pl.BlockSpec((1, 1, 1, rows), lambda s, g, h, n: (s, g * GROUP + h, 0, 0)),
                table,
                table,
            ],
            out_specs=[
                heads,
                pl.BlockSpec((2, 1, keys, HD), lambda s, g, h, n: (0, s, 0, g)),
            ],
            scratch_shapes=[
                pltpu.VMEM((keys, rows), F32),
                pltpu.VMEM((HD, keys), BF16),
                pltpu.VMEM((keys, HD), F32),
                pltpu.VMEM((keys, HD), F32),
            ],
        ),
        out_shape=[
            jax.ShapeDtypeStruct((seqs * rows, H * HD), BF16),
            jax.ShapeDtypeStruct((2, seqs, keys, KVH * HD), BF16),
        ],
        compiler_params=params(),
        cost_estimate=pl.CostEstimate(
            flops=10 * seqs * H * rows * keys * HD,
            bytes_accessed=4 * seqs * (2 * rows * H * HD + keys * 2 * KVH * HD),
            transcendentals=seqs * H * rows * keys,
        ),
        name="attend_back",
    )(lengths, qkv, keyval, keyval, posk, posq, grad, attended, lse, cosine, sine)


def route_kernel(
    att_ref, w_ref, x_ref, gain_ref, router_ref, hit_ref, middle_ref, first_ref, second_ref, gates_ref
):
    rows = x_ref.shape[0]
    experts = hit_ref.shape[0]
    middle = x_ref[...].astype(F32) + nn(att_ref[...], w_ref[...])
    middle_ref[...] = middle
    inverse = lax.rsqrt(jnp.mean(middle * middle, axis=-1, keepdims=True) + EPSILON)
    tokens = ((middle * inverse) * gain_ref[...]).astype(BF16)
    first_ref[...] = tokens[: rows // 2]
    second_ref[: rows // 2] = tokens[rows // 2 :]
    hit = hit_ref[...] > 0
    logits = jnp.where(hit, nt(router_ref[...], tokens), NEG_FILL)
    raised = jnp.where(hit, jnp.exp(logits - jnp.max(logits, axis=0, keepdims=True)), 0.0)
    gates = raised / jnp.sum(raised, axis=0, keepdims=True)
    gates_ref[...] = gates
    coarse = gates.astype(BF16)
    fine = (gates - coarse.astype(F32)).astype(BF16)
    second_ref[rows // 2 :, :rows] = coarse
    second_ref[rows // 2 :, rows : 2 * rows] = fine
    second_ref[rows // 2 :, 2 * rows :] = jnp.zeros(
        (experts, second_ref.shape[1] - 2 * rows), BF16
    )


def route(attended, weight, x, gain, router, hit):
    rows, width = x.shape
    experts = hit.shape[0]
    return pl.pallas_call(
        route_kernel,
        out_shape=[
            jax.ShapeDtypeStruct((rows, width), F32),
            jax.ShapeDtypeStruct((rows // 2, width), BF16),
            jax.ShapeDtypeStruct((rows // 2 + experts, width), BF16),
            jax.ShapeDtypeStruct((experts, rows), F32),
        ],
        compiler_params=params(),
        cost_estimate=pl.CostEstimate(
            flops=2 * rows * width * (width + HD),
            bytes_accessed=2 * width * (width + 5 * rows),
            transcendentals=experts * rows,
        ),
        name="route",
    )(attended, weight, x, gain, router, hit)


def expert_kernel(
    cap, ids_ref, tok_a, tok_b, cot_a, cot_b, win_ref, wout_ref, *refs
):
    x_ref, active_ref, both_ref, grad_ref, mix_ref, back_ref = refs[-6:]
    number = pl.program_id(1)
    mine = ids_ref[number]
    half = tok_a.shape[1]
    rows = 2 * half
    experts = tok_b.shape[1] - half
    width = tok_a.shape[2]
    row_is_mine = lax.broadcasted_iota(jnp.int32, (experts, 1), 0) == mine

    def own_row(values):
        return jnp.sum(jnp.where(row_is_mine, values.astype(F32), 0.0), axis=0, keepdims=True)

    hits, spreads, gates, picked, grads = [], [], [], [], []
    for g in range(2):
        slot = own_row(cot_b[g, half:, :rows]).astype(jnp.int32)
        gate_row = own_row(
            tok_b[g, half:, :rows].astype(F32) + tok_b[g, half:, rows : 2 * rows].astype(F32)
        )
        hit = lax.broadcasted_iota(jnp.int32, (cap, rows), 0) == slot
        spread = jnp.where(hit, 1.0, 0.0).astype(BF16)
        hits.append(hit)
        spreads.append(spread)
        gates.append(jnp.sum(jnp.where(hit, gate_row, 0.0), axis=1, keepdims=True))
        picked.append(nn(spread[:, :half], tok_a[g]) + nn(spread[:, half:], tok_b[g, :half]))
        grads.append(nn(spread[:, :half], cot_a[g]) + nn(spread[:, half:], cot_b[g, :half]))
    tokens = jnp.concatenate(picked, axis=0).astype(BF16)
    grad_out = jnp.concatenate(grads, axis=0)
    gate = jnp.concatenate(gates, axis=0)
    x_ref[0, 0] = tokens.reshape(2, cap, width)
    both = nn(tokens, win_ref[0])
    gate_part, up_part = both[:, :FF], both[:, FF:]
    sigmoid = 1.0 / (1.0 + jnp.exp(-gate_part))
    silu = gate_part * sigmoid
    active = (silu * up_part).astype(BF16)
    active_ref[0, 0] = active.reshape(2, cap, FF)
    produced = nn(active, wout_ref[0]).astype(BF16).astype(F32)
    grad_gate = jnp.sum(produced * grad_out, axis=1, keepdims=True)
    weighed = (produced * gate).astype(BF16)
    grad_produced = (grad_out * gate).astype(BF16)
    grad_ref[0, 0] = grad_produced.reshape(2, cap, width)
    grad_active = nt(grad_produced, wout_ref[0])
    grad_both = jnp.concatenate(
        [
            grad_active * up_part * sigmoid * (1.0 + gate_part * (1.0 - sigmoid)),
            grad_active * silu,
        ],
        axis=1,
    ).astype(BF16)
    both_ref[0, 0] = grad_both.reshape(2, cap, 2 * FF)
    grad_rows = nt(grad_both, win_ref[0]).astype(BF16)

    @pl.when(number == 0)
    def _():
        mix_ref[...] = jnp.zeros_like(mix_ref)
        back_ref[...] = jnp.zeros_like(back_ref)

    for g in range(2):
        part = slice(g * cap, (g + 1) * cap)
        mix_ref[g] = (mix_ref[g].astype(F32) + tn(spreads[g], weighed[part])).astype(BF16)
        back_ref[g, :rows] = (
            back_ref[g, :rows].astype(F32) + tn(spreads[g], grad_rows[part])
        ).astype(BF16)
        dense = jnp.sum(jnp.where(hits[g], grad_gate[part], 0.0), axis=0, keepdims=True)
        coarse = dense.astype(BF16).astype(F32)
        fine = dense - coarse
        back_ref[g, rows:, :rows] += jnp.where(row_is_mine, coarse, 0.0).astype(BF16)
        back_ref[g, rows:, rows : 2 * rows] += jnp.where(row_is_mine, fine, 0.0).astype(BF16)


def experts_step(ids, cap, side, tok_a, tok_b, cot_a, cot_b, win, wout, earlier):
    n_low, half, width = tok_a.shape
    experts = tok_b.shape[1] - half
    local = win.shape[0]
    tokens = lambda n: pl.BlockSpec((2, n, width), lambda i, j, ids: (i, 0, 0))
    rows = lambda n: pl.BlockSpec((1, 1, 2, cap, n), lambda i, j, ids: (j, side, i, 0, 0))
    rows_shape = lambda n: jax.ShapeDtypeStruct((local, 2, n_low, cap, n), BF16)
    earlier = tuple(earlier)
    n_rows = local * n_low * cap
    return pl.pallas_call(
        functools.partial(expert_kernel, cap),
        grid_spec=pltpu.PrefetchScalarGridSpec(
            num_scalar_prefetch=1,
            grid=(n_low // 2, local),
            in_specs=[
                tokens(half),
                tokens(half + experts),
                tokens(half),
                tokens(half + experts),
                pl.BlockSpec((1,) + win.shape[1:], lambda i, j, ids: (j, 0, 0)),
                pl.BlockSpec((1,) + wout.shape[1:], lambda i, j, ids: (j, 0, 0)),
            ]
            + [pl.BlockSpec(memory_space=pl.ANY)] * len(earlier),
            out_specs=[
                rows(width),
                rows(FF),
                rows(2 * FF),
                rows(width),
                tokens(2 * half),
                tokens(2 * half + experts),
            ],
        ),
        out_shape=[
            rows_shape(width),
            rows_shape(FF),
            rows_shape(2 * FF),
            rows_shape(width),
            jax.ShapeDtypeStruct((n_low, 2 * half, width), BF16),
            jax.ShapeDtypeStruct((n_low, 2 * half + experts, width), BF16),
        ],
        input_output_aliases={7 + k: k for k in range(len(earlier))},
        compiler_params=params(),
        cost_estimate=pl.CostEstimate(
            flops=n_rows * (12 * width * FF + 16 * half * width),
            bytes_accessed=2 * (n_low * half * width * 8 + n_rows * 4 * width + 6 * FF * width * local),
            transcendentals=n_rows * FF,
        ),
        name="experts",
    )(ids, tok_a, tok_b, cot_a, cot_b, win, wout, *earlier)


def unroute_kernel(
    first_ref, second_ref, gates_ref, middle_ref, gain_ref, router_ref, cot_ref, w_ref,
    grad_ref, branch_ref, att_ref, router_grad_ref, gain_grad_ref,
):
    rows = middle_ref.shape[0]
    half = rows // 2
    gates = gates_ref[...]
    grad_gate = second_ref[half:, :rows].astype(F32) + second_ref[half:, rows : 2 * rows].astype(F32)
    grad_logits = gates * (grad_gate - jnp.sum(gates * grad_gate, axis=0, keepdims=True))
    middle = middle_ref[...]
    inverse = lax.rsqrt(jnp.mean(middle * middle, axis=-1, keepdims=True) + EPSILON)
    normed = middle * inverse
    tokens = (normed * gain_ref[...]).astype(BF16).astype(F32)
    router_grad_ref[...] = nn(grad_logits, tokens, HIGHEST)
    grad_tokens = jnp.concatenate([first_ref[...], second_ref[:half]], axis=0).astype(F32)
    grad_tokens = grad_tokens + nn(grad_logits.T, router_ref[...].astype(F32), HIGHEST)
    gain_grad_ref[...] = jnp.sum(grad_tokens * normed, axis=0, keepdims=True)
    grad_middle = cot_ref[...].astype(F32) + norm_back(grad_tokens, gain_ref[...], normed, inverse)
    grad_ref[...] = grad_middle
    branch = grad_middle.astype(BF16)
    branch_ref[...] = branch
    att_ref[...] = nt(branch, w_ref[...]).astype(BF16)


def unroute(first, second, gates, middle, gain, router, cotangent, weight):
    rows, width = middle.shape
    experts = gates.shape[0]
    return pl.pallas_call(
        unroute_kernel,
        out_shape=[
            jax.ShapeDtypeStruct((rows, width), F32),
            jax.ShapeDtypeStruct((rows, width), BF16),
            jax.ShapeDtypeStruct((rows, width), BF16),
            jax.ShapeDtypeStruct((experts, width), F32),
            jax.ShapeDtypeStruct((1, width), F32),
        ],
        compiler_params=params(),
        cost_estimate=pl.CostEstimate(
            flops=2 * rows * width * (width + HD),
            bytes_accessed=2 * width * (width + 8 * rows),
            transcendentals=0,
        ),
        name="unroute",
    )(first, second, gates, middle, gain, router, cotangent, weight)


def unproject_kernel(
    x_ref, gain_ref, grad_ref, dq_ref, dkv_ref, w_ref, cos_ref, sin_ref, out_ref, dkv_raw_ref, gain_grad_ref
):
    rows, width = x_ref.shape
    for k in range(KVH):
        part = slice(k * HD, (k + 1) * HD)
        dkv_raw_ref[:, part] = turn(
            dkv_ref[0, :, part].astype(F32), cos_ref[...], -sin_ref[...]
        ).astype(BF16)
    dkv_raw_ref[:, KVH * HD :] = dkv_ref[1]
    n_query = dq_ref.shape[1]
    grad_hidden = nt(dq_ref[...], w_ref[:, :n_query]) + nt(dkv_raw_ref[...], w_ref[:, n_query:])
    x = x_ref[...].astype(F32)
    inverse = lax.rsqrt(jnp.mean(x * x, axis=-1, keepdims=True) + EPSILON)
    normed = x * inverse
    gain_grad_ref[...] = jnp.sum(grad_hidden * normed, axis=0, keepdims=True)
    out_ref[...] = (
        grad_ref[...] + norm_back(grad_hidden, gain_ref[...], normed, inverse)
    ).astype(BF16)


def unproject(x, gain, grad_middle, dq, dkv, weight, cosine, sine):
    rows, width = x.shape
    return pl.pallas_call(
        unproject_kernel,
        out_shape=[
            jax.ShapeDtypeStruct((rows, width), BF16),
            jax.ShapeDtypeStruct((rows, 2 * KVH * HD), BF16),
            jax.ShapeDtypeStruct((1, width), F32),
        ],
        compiler_params=params(),
        cost_estimate=pl.CostEstimate(
            flops=2 * rows * width * weight.shape[1],
            bytes_accessed=2 * width * (weight.shape[1] + 5 * rows),
            transcendentals=0,
        ),
        name="unproject",
    )(x, gain, grad_middle, dq, dkv, weight, cosine, sine)


def place_blocks(block_order, storage, sub_len):
    blocks = storage // sub_len
    matches = blocks[:, None] == jnp.arange(block_order.shape[0], dtype=jnp.int32)[None, :]
    return (
        jnp.sum(jnp.where(matches, block_order[None, :], 0), axis=1) * sub_len + storage % sub_len
    )


def per_device(
    layer_input,
    cotangent,
    seq_lengths,
    routes,
    drop_order,
    block_order,
    attn_gain,
    query_weight,
    keyval_weight,
    output_weight,
    moe_gain,
    router_weight,
    expert_in,
    expert_out,
):
    seqs, block_len, width = layer_input.shape
    core, high = lax.axis_index("c"), lax.axis_index("h")
    top, low = lax.axis_index("t"), lax.axis_index("l")
    n_high, n_low = lax.axis_size("h"), lax.axis_size("l")
    ctx_size, shard_size = 2 * n_high, 2 * n_low
    rows = seqs * block_len
    seq_len = block_len * ctx_size
    local = expert_in.shape[0]
    experts = local * shard_size
    cap = (5 * rows * TOPK + 4 * experts - 1) // (4 * experts)
    half = rows // 2

    small = jnp.concatenate([attn_gain[:, None], moe_gain[:, None], router_weight], axis=1)
    small = jnp.pad(small, ((0, 0), (0, HD - small.shape[1])))
    first_pack = jnp.concatenate([query_weight, keyval_weight, small], axis=1)

    def gather_weight(part):
        own = pick(part.reshape(2, part.shape[0] // 2, part.shape[1]), core, 0)
        return lax.all_gather(own, ("t", "l", "c"), axis=0, tiled=True)

    first_full = gather_weight(first_pack)
    output_full = gather_weight(output_weight)
    n_qkv = query_weight.shape[1] + keyval_weight.shape[1]
    qkv_full = first_full[:, :n_qkv]
    small_full = first_full[:, n_qkv:].T
    attn_scale = small_full[0:1].astype(F32)
    moe_scale = small_full[1:2].astype(F32)
    router_full = small_full[2 : 2 + experts]

    sub_len = seq_len // block_order.shape[0]
    inner = jnp.arange(block_len, dtype=jnp.int32)
    local_pos = place_blocks(block_order, (high * 2 + core) * block_len + inner, sub_len)
    relative = jnp.arange(ctx_size, dtype=jnp.int32)
    key_ctx = ((relative // 2) ^ high) * 2 + ((relative % 2) ^ core)
    key_pos = place_blocks(
        block_order, (key_ctx[:, None] * block_len + inner[None, :]).reshape(-1), sub_len
    )
    live = (local_pos[None, :] < seq_lengths[:, None]).reshape(rows)
    token_routes = routes.reshape(rows, TOPK).T
    hit = jnp.any(
        token_routes[None, :, :] == jnp.arange(experts, dtype=jnp.int32)[:, None, None], axis=1
    )
    load = hit & live[None, :]
    seq_ids = jnp.repeat(jnp.arange(seqs, dtype=jnp.int32), block_len)
    priority = drop_order.reshape(rows) * seqs + seq_ids
    earlier = (priority[:, None] < priority[None, :]).astype(BF16)
    ahead = jnp.dot(load.astype(BF16), earlier, preferred_element_type=F32)
    slots = jnp.where(load & (ahead < cap), ahead, -1.0).astype(BF16)

    angles = local_pos.astype(F32)[:, None] * (
        ROPE_BASE ** (-2.0 * jnp.arange(HD // 2, dtype=F32) / HD)
    )
    cosine, sine = jnp.cos(angles), jnp.sin(angles)
    cosine = jnp.concatenate([cosine, cosine], axis=1)
    sine = jnp.concatenate([-sine, sine], axis=1)
    cosine_rows, sine_rows = jnp.tile(cosine, (seqs, 1)), jnp.tile(sine, (seqs, 1))

    win = gather_expert(expert_in)
    wout = gather_expert(expert_out)

    x = layer_input.reshape(rows, width)
    hidden, qkv = project(x, attn_scale, qkv_full, cosine_rows, sine_rows)
    keyval = qkv[:, H * HD :].reshape(seqs, 1, 1, block_len, 2 * KVH * HD)
    for bit in bits_of("h"):
        keyval = jnp.concatenate([keyval, swap(keyval, "h", bit)], axis=1)
    keyval = jnp.concatenate([keyval, swap(keyval, "c")], axis=2)
    keyval = keyval.reshape(seqs, seq_len, 2 * KVH * HD)
    posk, posq = key_pos[:, None], local_pos[None, :]
    attended, lse = attend(seq_lengths, qkv, keyval, posk, posq)
    middle, tok_a, tok_b, gates = route(
        attended, output_full, x, moe_scale, router_full, hit.astype(F32)
    )

    grad_out = cotangent.reshape(rows, width) * live[:, None].astype(BF16)
    extra = jnp.pad(slots, ((0, 0), (0, width - rows)))
    cot_b = jnp.concatenate([grad_out[half:], extra], axis=0)
    cot_a, cot_b, _ = lax.optimization_barrier((grad_out[:half], cot_b, qkv))

    def to_group(part_a, part_b):
        near_a, near_b = gather_group(part_a, True), gather_group(part_b, False)
        return (near_a, near_b), (swap(near_a, "c"), swap(near_b, "c"))

    cot_near, cot_far = to_group(cot_a, cot_b)
    tok_near, tok_far = to_group(tok_a, tok_b)

    number = jnp.arange(local, dtype=jnp.int32)
    per_core = local // 2
    ids = ((top ^ (number // per_core)) * n_low + low) * local + core * per_core + number % per_core
    step = functools.partial(experts_step, ids, cap)
    *saved, mix_near, back_near = step(0, *tok_near, *cot_near, win, wout, ())
    *saved, mix_far, back_far = step(1, *tok_far, *cot_far, win, wout, saved)
    picked, active, grad_both, grad_produced = (
        s.reshape(local, 2 * n_low * cap, s.shape[-1]) for s in saved
    )

    def from_group(near, far):
        total = add_low(near, swap(far, "c"))
        return reduce_group(total[:, :half], True), reduce_group(total[:, half:], False)

    back_a, back_b = from_group(back_near, back_far)
    mix_near, mix_far, _ = lax.optimization_barrier((mix_near, mix_far, back_a))
    mix_a, mix_b = from_group(mix_near, mix_far)
    output = (middle + jnp.concatenate([mix_a, mix_b], axis=0).astype(F32)).astype(BF16)

    grad_expert_out = jnp.einsum(
        "erf,erd->efd", active, grad_produced, preferred_element_type=F32
    ).astype(BF16)
    grad_expert_in = jnp.einsum(
        "erd,erf->edf", picked, grad_both, preferred_element_type=F32
    ).astype(BF16)
    expert_out_sum = reduce_expert(grad_expert_out, local)
    expert_in_sum = reduce_expert(grad_expert_in, local)

    grad_middle, branch, grad_attended, router_grad, moe_gain_grad = unroute(
        back_a, back_b, gates, middle, moe_scale, router_full, grad_out, output_full
    )
    grad_output_weight = jnp.dot(attended.T, branch, preferred_element_type=F32).astype(BF16)
    output_sum = reduce_weight(grad_output_weight)
    dq, dkv = attend_back(
        seq_lengths, qkv, keyval, posk, posq, grad_attended, attended, lse, cosine, sine
    )
    grad_query_weight = jnp.dot(hidden.T, dq, preferred_element_type=F32).astype(BF16)
    query_sum = reduce_weight(grad_query_weight)
    dkv = dkv.reshape(2, seqs, n_high, 2, block_len, KVH * HD)
    dkv = add_low(dkv[:, :, :, 0], swap(dkv[:, :, :, 1], "c"))
    for bit in reversed(bits_of("h")):
        count = dkv.shape[2] // 2
        dkv = add_low(dkv[:, :, :count], swap(dkv[:, :, count:], "h", bit))
    dkv = dkv.reshape(2, rows, KVH * HD)
    grad_input, dkv_raw, attn_gain_grad = unproject(
        x, attn_scale, grad_middle, dq, dkv, qkv_full, cosine_rows, sine_rows
    )
    grad_keyval_weight = jnp.dot(hidden.T, dkv_raw, preferred_element_type=F32).astype(BF16)
    small_grad = jnp.concatenate([attn_gain_grad, moe_gain_grad, router_grad], axis=0)
    small_grad = jnp.pad(small_grad, ((0, HD - small_grad.shape[0]), (0, 0))).astype(BF16).T
    last_sum = reduce_weight(jnp.concatenate([grad_keyval_weight, small_grad], axis=1))
    n_kv = keyval_weight.shape[1]
    shape = (seqs, block_len, width)
    return (
        output.reshape(shape),
        grad_input.reshape(shape),
        last_sum[:, n_kv],
        query_sum,
        last_sum[:, :n_kv],
        output_sum,
        last_sum[:, n_kv + 1],
        last_sum[:, n_kv + 2 : n_kv + 2 + experts],
        expert_in_sum,
        expert_out_sum,
    )


def solution(mesh):
    ctx, shard = mesh.shape["ctx"], mesh.shape["shard"]
    cut = Mesh(mesh.devices.reshape(ctx // 2, 2, 2, shard // 2), ("h", "c", "t", "l"))
    c, s = ("h", "c"), ("t", "l")
    placed = (
        P(s, c, None),
        P(s, c, None),
        P(s),
        P(s, c, None),
        P(s, c),
        P(),
        P(s),
        P(s, None),
        P(s, None),
        P(s, None),
        P(s),
        P(s, None),
        P(s, c, None),
        P(s, c, None),
    )
    return jax.shard_map(
        per_device,
        mesh=cut,
        in_specs=placed,
        out_specs=(
            P(s, c, None),
            P(s, c, None),
            P(s),
            P(s, None),
            P(s, None),
            P(s, None),
            P(s),
            P(s, None),
            P(s, c, None),
            P(s, c, None),
        ),
        check_vma=False,
    )
```

```python
import functools

import jax
import jax.numpy as jnp
from jax import lax
from jax.experimental import pallas as pl
from jax.experimental.pallas import tpu as pltpu
from jax.sharding import Mesh
from jax.sharding import PartitionSpec as P

H = 12
KVH = 2
HD = 128
FF = 768
TOPK = 4
GROUP = H // KVH

EPSILON = 1e-06
ROPE_BASE = 10000.0
HIGHEST = lax.Precision.HIGHEST
NEG_FILL = -1e30
LOG2E = 1.4426950408889634
SCALE = HD ** (-0.5)
VMEM_LIMIT = 60 * 1024 * 1024
SMALL = pl.CostEstimate(flops=1000, bytes_accessed=1000, transcendentals=0)
F32 = jnp.float32
BF16 = jnp.bfloat16


def params(limit=VMEM_LIMIT):
    return pltpu.CompilerParams(vmem_limit_bytes=limit)


def nt(a, b, precision=None):
    return lax.dot_general(
        a, b, (((1,), (1,)), ((), ())), precision=precision, preferred_element_type=F32
    )


def tn(a, b, precision=None):
    return lax.dot_general(
        a, b, (((0,), (0,)), ((), ())), precision=precision, preferred_element_type=F32
    )


def nn(a, b, precision=None):
    return jnp.dot(a, b, precision=precision, preferred_element_type=F32)


def swap(value, axis, bit=1):
    size = lax.axis_size(axis)
    return lax.ppermute(value, axis, [(i, i ^ bit) for i in range(size)])


def bits_of(axis):
    size = lax.axis_size(axis)
    return [1 << k for k in range(size.bit_length() - 1)]


def add_low(a, b):
    return (a.astype(F32) + b.astype(F32)).astype(BF16)


def pick(value, index, axis):
    return lax.dynamic_index_in_dim(value, index, axis, keepdims=False)


def after(value, *others):
    return lax.optimization_barrier((value,) + others)[0]


def sync(*values):
    return lax.optimization_barrier(values)


def low_axes(value):
    return value.reshape((2,) * len(bits_of("l")) + value.shape[1:])


def open_low(part):
    return part.reshape((1,) * len(bits_of("l")) + part.shape)


def gather_bit(value, k):
    bits = bits_of("l")
    return jnp.concatenate([value, swap(value, "l", bits[k])], axis=len(bits) - 1 - k)


def total_of(*parts):
    return sum(p.astype(F32) for p in parts).astype(BF16)


def reduce_bit(parts, k):
    bits = bits_of("l")
    axis = len(bits) - 1 - k
    send = total_of(*[lax.slice_in_dim(p, 1, 2, axis=axis) for p in parts])
    keep = [lax.slice_in_dim(p, 0, 1, axis=axis) for p in parts]
    return total_of(*keep, swap(send, "l", bits[k]))


def by_core(own, other, axis):
    return jnp.where(
        lax.axis_index("c") == 0,
        jnp.concatenate([own, other], axis=axis),
        jnp.concatenate([other, own], axis=axis),
    )


def spread_high(piece):
    pieces = [piece]
    for bit in bits_of("h"):
        pieces = pieces + [swap(p, "h", bit) for p in pieces]
    return pieces


def place_high(whole, far, pieces, first):
    high = lax.axis_index("h")
    for r, p in enumerate(pieces):
        whole = lax.dynamic_update_slice(whole, p[None, :, None], (far, 0, high ^ r, 0, first, 0))
    return whole


def joined(whole):
    return whole.reshape(whole.shape[0] * whole.shape[1], -1, whole.shape[-1])


def scatter_expert(grad, per_core):
    n_high = lax.axis_size("h")
    grad = grad.reshape(2, per_core, n_high, -1, grad.shape[-1])
    grad = jnp.swapaxes(grad, 1, 2)
    grad = grad.reshape((2 * n_high,) + grad.shape[2:])
    total = lax.psum_scatter(grad, ("t", "h"), scatter_dimension=0, tiled=True)
    return total.reshape(per_core, 2, -1, total.shape[-1])


def reduce_core(value):
    core = lax.axis_index("c")
    other = swap(pick(value, 1 - core, 1), "c")
    return by_core(pick(value, core, 1), other, 0).astype(F32)


def weight_core(grad):
    core, n_low = lax.axis_index("c"), lax.axis_size("l")
    value = grad.reshape(2, n_low, 2, -1, grad.shape[1])
    return add_low(pick(value, core, 2), swap(pick(value, 1 - core, 2), "c"))


def weight_low(value):
    value = lax.all_to_all(value, "l", split_axis=1, concat_axis=1, tiled=True)
    return jnp.sum(value.astype(F32), axis=1).astype(BF16)


def weight_bits(value):
    low = lax.axis_index("l")
    count = lax.axis_size("l")
    for bit in bits_of("l"):
        count //= 2
        value = value.reshape((2, count, 2) + value.shape[-2:])
        side = (low & bit) // bit
        value = add_low(pick(value, side, 2), swap(pick(value, 1 - side, 2), "l", bit))
    return value.reshape((2,) + value.shape[-2:])


def weight_top(value):
    top = lax.axis_index("t")
    return add_low(pick(value, top, 0), swap(pick(value, 1 - top, 0), "t"))


def weight_high(value):
    for bit in bits_of("h"):
        value = add_low(value, swap(value, "h", bit))
    return value


def weight_done(value):
    return by_core(value, swap(value, "c"), 0).astype(F32)


def norm_back(grad_normed, gain, normed, inverse):
    scaled = grad_normed * gain
    return inverse * (scaled - normed * jnp.mean(scaled * normed, axis=-1, keepdims=True))


def turn(values, cosine, sine):
    return values * cosine + pltpu.roll(values, HD // 2, 1) * sine


def project_kernel(x_ref, gain_ref, w_ref, cos_ref, sin_ref, hidden_ref, out_ref):
    step = pl.program_id(0)

    @pl.when(step == 0)
    def _():
        x = x_ref[...].astype(F32)
        inverse = lax.rsqrt(jnp.mean(x * x, axis=-1, keepdims=True) + EPSILON)
        hidden_ref[...] = ((x * inverse) * gain_ref[...]).astype(BF16)

    raw = nn(hidden_ref[...], w_ref[...])
    per_step = raw.shape[1] // HD
    for k in range(per_step):
        head = raw[:, k * HD : (k + 1) * HD]
        turned = turn(head, cos_ref[...], sin_ref[...])
        is_value = step * per_step + k >= H + KVH
        out_ref[:, k * HD : (k + 1) * HD] = jnp.where(is_value, head, turned).astype(BF16)


def project(x, gain, weight, cosine, sine):
    rows, width = x.shape
    columns = (H + 2 * KVH) * HD
    block = 512
    return pl.pallas_call(
        project_kernel,
        grid=(columns // block,),
        in_specs=[
            pl.BlockSpec((rows, width), lambda i: (0, 0)),
            pl.BlockSpec((1, width), lambda i: (0, 0)),
            pl.BlockSpec((width, block), lambda i: (0, i)),
            pl.BlockSpec((rows, HD), lambda i: (0, 0)),
            pl.BlockSpec((rows, HD), lambda i: (0, 0)),
        ],
        out_specs=[
            pl.BlockSpec((rows, width), lambda i: (0, 0)),
            pl.BlockSpec((rows, block), lambda i: (0, i)),
        ],
        out_shape=[
            jax.ShapeDtypeStruct((rows, width), BF16),
            jax.ShapeDtypeStruct((rows, columns), BF16),
        ],
        compiler_params=params(),
        cost_estimate=SMALL,
        name="project",
    )(x, gain, weight, cosine, sine)


def set_bias(len_ref, posk_ref, posq_ref, bias):
    seq = pl.program_id(0)

    @pl.when((pl.program_id(1) == 0) & (pl.program_id(2) == 0))
    def _():
        posk = posk_ref[...]
        allowed = (posk <= posq_ref[...]) & (posk < len_ref[seq])
        bias[...] = jnp.where(allowed, 0.0, NEG_FILL)


def attend_kernel(len_ref, q_ref, k_ref, v_ref, posk_ref, posq_ref, out_ref, lse_ref, bias, turned):
    set_bias(len_ref, posk_ref, posq_ref, bias)

    @pl.when(pl.program_id(2) == 0)
    def _():
        turned[...] = v_ref[0].T

    scores = nt(k_ref[0], q_ref[...]) * (SCALE * LOG2E) + bias[...]
    top = jnp.max(scores, axis=0, keepdims=True)
    weights = jnp.exp2(scores - top)
    total = jnp.sum(weights, axis=0, keepdims=True)
    mixed = nn(turned[...], weights.astype(BF16)) * (1.0 / total)
    out_ref[...] = mixed.T.astype(BF16)
    lse_ref[0, 0] = top + jnp.log2(total)


def attend(lengths, qkv, keyval, posk, posq):
    seqs, keys, _ = keyval.shape
    rows = qkv.shape[0] // seqs
    return pl.pallas_call(
        attend_kernel,
        grid_spec=pltpu.PrefetchScalarGridSpec(
            num_scalar_prefetch=1,
            grid=(seqs, KVH, GROUP),
            in_specs=[
                pl.BlockSpec((rows, HD), lambda s, g, h, n: (s, g * GROUP + h)),
                pl.BlockSpec((1, keys, HD), lambda s, g, h, n: (s, 0, g)),
                pl.BlockSpec((1, keys, HD), lambda s, g, h, n: (s, 0, KVH + g)),
                pl.BlockSpec((keys, 1), lambda s, g, h, n: (0, 0)),
                pl.BlockSpec((1, rows), lambda s, g, h, n: (0, 0)),
            ],
            out_specs=[
                pl.BlockSpec((rows, HD), lambda s, g, h, n: (s, g * GROUP + h)),
                pl.BlockSpec((1, 1, 1, rows), lambda s, g, h, n: (s, g * GROUP + h, 0, 0)),
            ],
            scratch_shapes=[pltpu.VMEM((keys, rows), F32), pltpu.VMEM((HD, keys), BF16)],
        ),
        out_shape=[
            jax.ShapeDtypeStruct((seqs * rows, H * HD), BF16),
            jax.ShapeDtypeStruct((seqs, H, 1, rows), F32),
        ],
        compiler_params=params(),
        cost_estimate=SMALL,
        name="attend",
    )(lengths, qkv, keyval, keyval, posk, posq)


def attend_back_kernel(
    len_ref, q_ref, k_ref, v_ref, posk_ref, posq_ref, grad_ref, out_ref, lse_ref, cos_ref, sin_ref,
    dq_ref, dkv_ref, bias, turned, dk, dv,
):
    set_bias(len_ref, posk_ref, posq_ref, bias)
    head = pl.program_id(2)

    @pl.when(head == 0)
    def _():
        turned[...] = k_ref[0].T
        dk[...] = jnp.zeros_like(dk)
        dv[...] = jnp.zeros_like(dv)

    q, grad = q_ref[...], grad_ref[...]
    scores = nt(k_ref[0], q) * (SCALE * LOG2E) + bias[...]
    probs = jnp.exp2(scores - lse_ref[0, 0])
    grad_probs = nt(v_ref[0], grad)
    product = grad.astype(F32) * out_ref[...].astype(F32)
    delta = jnp.sum(product.T, axis=0, keepdims=True)
    grad_scores = (probs * (grad_probs - delta)).astype(BF16)
    dv[...] += nn(probs.astype(BF16), grad)
    dk[...] += nn(grad_scores, q)
    dq = nn(turned[...], grad_scores).T * SCALE
    dq_ref[...] = turn(dq, cos_ref[...], -sin_ref[...]).astype(BF16)

    @pl.when(head == GROUP - 1)
    def _():
        dkv_ref[0, 0] = (dk[...] * SCALE).astype(BF16)
        dkv_ref[1, 0] = dv[...].astype(BF16)


def attend_back(lengths, qkv, keyval, posk, posq, grad, attended, lse, cosine, sine):
    seqs, keys, _ = keyval.shape
    rows = qkv.shape[0] // seqs
    heads = pl.BlockSpec((rows, HD), lambda s, g, h, n: (s, g * GROUP + h))
    table = pl.BlockSpec((rows, HD), lambda s, g, h, n: (0, 0))
    return pl.pallas_call(
        attend_back_kernel,
        grid_spec=pltpu.PrefetchScalarGridSpec(
            num_scalar_prefetch=1,
            grid=(seqs, KVH, GROUP),
            in_specs=[
                heads,
                pl.BlockSpec((1, keys, HD), lambda s, g, h, n: (s, 0, g)),
                pl.BlockSpec((1, keys, HD), lambda s, g, h, n: (s, 0, KVH + g)),
                pl.BlockSpec((keys, 1), lambda s, g, h, n: (0, 0)),
                pl.BlockSpec((1, rows), lambda s, g, h, n: (0, 0)),
                heads,
                heads,
                pl.BlockSpec((1, 1, 1, rows), lambda s, g, h, n: (s, g * GROUP + h, 0, 0)),
                table,
                table,
            ],
            out_specs=[
                heads,
                pl.BlockSpec((2, 1, keys, HD), lambda s, g, h, n: (0, s, 0, g)),
            ],
            scratch_shapes=[
                pltpu.VMEM((keys, rows), F32),
                pltpu.VMEM((HD, keys), BF16),
                pltpu.VMEM((keys, HD), F32),
                pltpu.VMEM((keys, HD), F32),
            ],
        ),
        out_shape=[
            jax.ShapeDtypeStruct((seqs * rows, H * HD), BF16),
            jax.ShapeDtypeStruct((2, seqs, keys, KVH * HD), BF16),
        ],
        compiler_params=params(),
        cost_estimate=SMALL,
        name="attend_back",
    )(lengths, qkv, keyval, keyval, posk, posq, grad, attended, lse, cosine, sine)


def route_kernel(
    att_ref, w_ref, x_ref, gain_ref, router_ref, hit_ref, middle_ref, first_ref, second_ref, gates_ref
):
    rows = x_ref.shape[0]
    experts = hit_ref.shape[0]
    middle = x_ref[...].astype(F32) + nn(att_ref[...], w_ref[...])
    middle_ref[...] = middle
    inverse = lax.rsqrt(jnp.mean(middle * middle, axis=-1, keepdims=True) + EPSILON)
    tokens = ((middle * inverse) * gain_ref[...]).astype(BF16)
    first_ref[...] = tokens[: rows // 2]
    second_ref[: rows // 2] = tokens[rows // 2 :]
    hit = hit_ref[...] > 0
    logits = jnp.where(hit, nt(router_ref[...], tokens), NEG_FILL)
    raised = jnp.where(hit, jnp.exp(logits - jnp.max(logits, axis=0, keepdims=True)), 0.0)
    gates = raised / jnp.sum(raised, axis=0, keepdims=True)
    gates_ref[...] = gates
    coarse = gates.astype(BF16)
    fine = (gates - coarse.astype(F32)).astype(BF16)
    second_ref[rows // 2 :, :rows] = coarse
    second_ref[rows // 2 :, rows : 2 * rows] = fine
    second_ref[rows // 2 :, 2 * rows :] = jnp.zeros(
        (experts, second_ref.shape[1] - 2 * rows), BF16
    )


def route(attended, weight, x, gain, router, hit):
    rows, width = x.shape
    experts = hit.shape[0]
    return pl.pallas_call(
        route_kernel,
        out_shape=[
            jax.ShapeDtypeStruct((rows, width), F32),
            jax.ShapeDtypeStruct((rows // 2, width), BF16),
            jax.ShapeDtypeStruct((rows // 2 + experts, width), BF16),
            jax.ShapeDtypeStruct((experts, rows), F32),
        ],
        compiler_params=params(),
        cost_estimate=SMALL,
        name="route",
    )(attended, weight, x, gain, router, hit)


def expert_kernel(
    cap, ids_ref, tok_a, tok_b, cot_a, cot_b, win_ref, wout_ref, *refs
):
    x_ref, active_ref, both_ref, grad_ref, mix_ref, back_a, back_b = refs[-7:]
    number = pl.program_id(1)
    mine = ids_ref[number]
    half = tok_a.shape[1]
    rows = 2 * half
    experts = tok_b.shape[1] - half
    width = tok_a.shape[2]
    row_is_mine = lax.broadcasted_iota(jnp.int32, (experts, 1), 0) == mine

    def own_row(values):
        return jnp.sum(jnp.where(row_is_mine, values.astype(F32), 0.0), axis=0, keepdims=True)

    hits, spreads, gates, picked, grads = [], [], [], [], []
    for g in range(2):
        slot = own_row(cot_b[g, half:, :rows]).astype(jnp.int32)
        gate_row = own_row(
            tok_b[g, half:, :rows].astype(F32) + tok_b[g, half:, rows : 2 * rows].astype(F32)
        )
        hit = lax.broadcasted_iota(jnp.int32, (cap, rows), 0) == slot
        spread = jnp.where(hit, 1.0, 0.0).astype(BF16)
        hits.append(hit)
        spreads.append(spread)
        gates.append(jnp.sum(jnp.where(hit, gate_row, 0.0), axis=1, keepdims=True))
        picked.append(nn(spread[:, :half], tok_a[g]) + nn(spread[:, half:], tok_b[g, :half]))
        grads.append(nn(spread[:, :half], cot_a[g]) + nn(spread[:, half:], cot_b[g, :half]))
    tokens = jnp.concatenate(picked, axis=0).astype(BF16)
    grad_out = jnp.concatenate(grads, axis=0)
    gate = jnp.concatenate(gates, axis=0)
    x_ref[0, 0] = tokens.reshape(2, cap, width)
    both = nn(tokens, win_ref[0])
    gate_part, up_part = both[:, :FF], both[:, FF:]
    sigmoid = 1.0 / (1.0 + jnp.exp(-gate_part))
    silu = gate_part * sigmoid
    active = (silu * up_part).astype(BF16)
    active_ref[0, 0] = active.reshape(2, cap, FF)
    produced = nn(active, wout_ref[0]).astype(BF16).astype(F32)
    grad_gate = jnp.sum(produced * grad_out, axis=1, keepdims=True)
    weighed = (produced * gate).astype(BF16)
    grad_produced = (grad_out * gate).astype(BF16)
    grad_ref[0, 0] = grad_produced.reshape(2, cap, width)
    grad_active = nt(grad_produced, wout_ref[0])
    grad_both = jnp.concatenate(
        [
            grad_active * up_part * sigmoid * (1.0 + gate_part * (1.0 - sigmoid)),
            grad_active * silu,
        ],
        axis=1,
    ).astype(BF16)
    both_ref[0, 0] = grad_both.reshape(2, cap, 2 * FF)
    grad_rows = nt(grad_both, win_ref[0]).astype(BF16)

    @pl.when(number == 0)
    def _():
        mix_ref[...] = jnp.zeros_like(mix_ref)
        back_a[...] = jnp.zeros_like(back_a)
        back_b[...] = jnp.zeros_like(back_b)

    for g in range(2):
        part = slice(g * cap, (g + 1) * cap)
        mix_ref[g] = (mix_ref[g].astype(F32) + tn(spreads[g], weighed[part])).astype(BF16)
        back = tn(spreads[g], grad_rows[part])
        back_a[g] = (back_a[g].astype(F32) + back[:half]).astype(BF16)
        back_b[g, :half] = (back_b[g, :half].astype(F32) + back[half:]).astype(BF16)
        dense = jnp.sum(jnp.where(hits[g], grad_gate[part], 0.0), axis=0, keepdims=True)
        coarse = dense.astype(BF16).astype(F32)
        fine = dense - coarse
        back_b[g, half:, :rows] += jnp.where(row_is_mine, coarse, 0.0).astype(BF16)
        back_b[g, half:, rows : 2 * rows] += jnp.where(row_is_mine, fine, 0.0).astype(BF16)


def experts_step(ids, cap, side, tok_a, tok_b, cot_a, cot_b, win, wout, earlier):
    n_low, half, width = tok_a.shape
    experts = tok_b.shape[1] - half
    local = win.shape[0]
    tokens = lambda n: pl.BlockSpec((2, n, width), lambda i, j, ids: (i, 0, 0))
    rows = lambda n: pl.BlockSpec(
        (1, 1, 2, cap, n), lambda i, j, ids: (ids[local + j], side, i, 0, 0)
    )
    rows_shape = lambda n: jax.ShapeDtypeStruct((local, 2, n_low, cap, n), BF16)
    weights = lambda w: pl.BlockSpec((1,) + w.shape[1:], lambda i, j, ids: (j, 0, 0))
    earlier = tuple(earlier)
    n_rows = local * n_low * cap
    return pl.pallas_call(
        functools.partial(expert_kernel, cap),
        grid_spec=pltpu.PrefetchScalarGridSpec(
            num_scalar_prefetch=1,
            grid=(n_low // 2, local),
            in_specs=[
                tokens(half),
                tokens(half + experts),
                tokens(half),
                tokens(half + experts),
                weights(win),
                weights(wout),
            ]
            + [pl.BlockSpec(memory_space=pl.ANY)] * len(earlier),
            out_specs=[
                rows(width),
                rows(FF),
                rows(2 * FF),
                rows(width),
                tokens(2 * half),
                tokens(half),
                tokens(half + experts),
            ],
        ),
        out_shape=[
            rows_shape(width),
            rows_shape(FF),
            rows_shape(2 * FF),
            rows_shape(width),
            jax.ShapeDtypeStruct((n_low, 2 * half, width), BF16),
            jax.ShapeDtypeStruct((n_low, half, width), BF16),
            jax.ShapeDtypeStruct((n_low, half + experts, width), BF16),
        ],
        input_output_aliases={7 + k: k for k in range(len(earlier))},
        compiler_params=params(),
        cost_estimate=SMALL,
        name="experts",
    )(ids, tok_a, tok_b, cot_a, cot_b, win, wout, *earlier)


def unroute_kernel(
    first_ref, second_ref, gates_ref, middle_ref, gain_ref, router_ref, cot_ref, w_ref,
    grad_ref, branch_ref, att_ref, router_grad_ref, gain_grad_ref,
):
    rows = middle_ref.shape[0]
    half = rows // 2
    gates = gates_ref[...]
    grad_gate = second_ref[half:, :rows].astype(F32) + second_ref[half:, rows : 2 * rows].astype(F32)
    grad_logits = gates * (grad_gate - jnp.sum(gates * grad_gate, axis=0, keepdims=True))
    middle = middle_ref[...]
    inverse = lax.rsqrt(jnp.mean(middle * middle, axis=-1, keepdims=True) + EPSILON)
    normed = middle * inverse
    tokens = (normed * gain_ref[...]).astype(BF16).astype(F32)
    router_grad_ref[...] = nn(grad_logits, tokens, HIGHEST)
    grad_tokens = jnp.concatenate([first_ref[...], second_ref[:half]], axis=0).astype(F32)
    grad_tokens = grad_tokens + nn(grad_logits.T, router_ref[...].astype(F32), HIGHEST)
    gain_grad_ref[...] = jnp.sum(grad_tokens * normed, axis=0, keepdims=True)
    grad_middle = cot_ref[...].astype(F32) + norm_back(grad_tokens, gain_ref[...], normed, inverse)
    grad_ref[...] = grad_middle
    branch = grad_middle.astype(BF16)
    branch_ref[...] = branch
    att_ref[...] = nt(branch, w_ref[...]).astype(BF16)


def unroute(first, second, gates, middle, gain, router, cotangent, weight):
    rows, width = middle.shape
    experts = gates.shape[0]
    return pl.pallas_call(
        unroute_kernel,
        out_shape=[
            jax.ShapeDtypeStruct((rows, width), F32),
            jax.ShapeDtypeStruct((rows, width), BF16),
            jax.ShapeDtypeStruct((rows, width), BF16),
            jax.ShapeDtypeStruct((experts, width), F32),
            jax.ShapeDtypeStruct((1, width), F32),
        ],
        compiler_params=params(),
        cost_estimate=SMALL,
        name="unroute",
    )(first, second, gates, middle, gain, router, cotangent, weight)


def unproject_kernel(
    x_ref, gain_ref, grad_ref, dq_ref, dkv_ref, w_ref, cos_ref, sin_ref, out_ref, dkv_raw_ref, gain_grad_ref
):
    rows, width = x_ref.shape
    for k in range(KVH):
        part = slice(k * HD, (k + 1) * HD)
        dkv_raw_ref[:, part] = turn(
            dkv_ref[0, :, part].astype(F32), cos_ref[...], -sin_ref[...]
        ).astype(BF16)
    dkv_raw_ref[:, KVH * HD :] = dkv_ref[1]
    n_query = dq_ref.shape[1]
    grad_hidden = nt(dq_ref[...], w_ref[:, :n_query]) + nt(
        dkv_raw_ref[...], w_ref[:, n_query : n_query + 2 * KVH * HD]
    )
    x = x_ref[...].astype(F32)
    inverse = lax.rsqrt(jnp.mean(x * x, axis=-1, keepdims=True) + EPSILON)
    normed = x * inverse
    gain_grad_ref[...] = jnp.sum(grad_hidden * normed, axis=0, keepdims=True)
    out_ref[...] = (
        grad_ref[...] + norm_back(grad_hidden, gain_ref[...], normed, inverse)
    ).astype(BF16)


def unproject(x, gain, grad_middle, dq, dkv, weight, cosine, sine):
    rows, width = x.shape
    return pl.pallas_call(
        unproject_kernel,
        out_shape=[
            jax.ShapeDtypeStruct((rows, width), BF16),
            jax.ShapeDtypeStruct((rows, 2 * KVH * HD), BF16),
            jax.ShapeDtypeStruct((1, width), F32),
        ],
        compiler_params=params(),
        cost_estimate=SMALL,
        name="unproject",
    )(x, gain, grad_middle, dq, dkv, weight, cosine, sine)


def place_blocks(block_order, storage, sub_len):
    blocks = storage // sub_len
    matches = blocks[:, None] == jnp.arange(block_order.shape[0], dtype=jnp.int32)[None, :]
    return (
        jnp.sum(jnp.where(matches, block_order[None, :], 0), axis=1) * sub_len + storage % sub_len
    )


def per_device(
    layer_input,
    cotangent,
    seq_lengths,
    routes,
    drop_order,
    block_order,
    attn_gain,
    query_weight,
    keyval_weight,
    output_weight,
    moe_gain,
    router_weight,
    expert_in,
    expert_out,
):
    seqs, block_len, width = layer_input.shape
    core, high = lax.axis_index("c"), lax.axis_index("h")
    top, low = lax.axis_index("t"), lax.axis_index("l")
    n_high, n_low = lax.axis_size("h"), lax.axis_size("l")
    ctx_size, shard_size = 2 * n_high, 2 * n_low
    rows = seqs * block_len
    seq_len = block_len * ctx_size
    local = expert_in.shape[0]
    experts = local * shard_size
    cap = (5 * rows * TOPK + 4 * experts - 1) // (4 * experts)
    half = rows // 2

    n_in, n_out = expert_in.shape[1], expert_out.shape[1]
    per_core = local // 2
    packed = jnp.concatenate([expert_in, expert_out], axis=1)
    own = lax.dynamic_slice_in_dim(packed, core * per_core, per_core, 0)
    away = lax.dynamic_slice_in_dim(packed, (1 - core) * per_core, per_core, 0)
    other = swap(away, "c")
    pair = by_core(own[:, None], other[:, None], 1)
    near = spread_high(pair)
    unit = (n_in + n_out) // 18
    cuts = [k * unit for k in (0, 6, 10, 12)] + [n_in + n_out]
    far_piece = lambda k: swap(pair[:, :, cuts[k] : cuts[k + 1]], "t")
    empty = lambda n: jnp.zeros((2, per_core, n_high, 2, n, width), BF16)

    def place(whole, far, pieces, first):
        count = pieces[0].shape[2]
        split = min(max(n_in - first, 0), count)
        if split > 0:
            whole = (place_high(whole[0], far, [p[:, :, :split] for p in pieces], first), whole[1])
        if split < count:
            rest = [p[:, :, split:] for p in pieces]
            whole = (whole[0], place_high(whole[1], far, rest, first + split - n_in))
        return whole

    far_0 = far_piece(0)

    small = jnp.concatenate([attn_gain[:, None], moe_gain[:, None], router_weight], axis=1)
    small = jnp.pad(small, ((0, 0), (0, HD - small.shape[1])))
    n_q, n_kv = query_weight.shape[1], keyval_weight.shape[1]

    def gather_weight(part):
        own = pick(part.reshape(2, -1, part.shape[1]), core, 0)
        return lax.all_gather(own, ("t", "l", "c"), axis=0, tiled=True)

    first_full = gather_weight(
        after(jnp.concatenate([query_weight, keyval_weight, small], axis=1), other)
    )

    sub_len = seq_len // block_order.shape[0]
    inner = jnp.arange(block_len, dtype=jnp.int32)
    local_pos = place_blocks(block_order, (high * 2 + core) * block_len + inner, sub_len)
    relative = jnp.arange(ctx_size, dtype=jnp.int32)
    key_ctx = ((relative // 2) ^ high) * 2 + ((relative % 2) ^ core)
    key_pos = place_blocks(
        block_order, (key_ctx[:, None] * block_len + inner[None, :]).reshape(-1), sub_len
    )
    live = (local_pos[None, :] < seq_lengths[:, None]).reshape(rows)
    token_routes = routes.reshape(rows, TOPK).T
    hit = jnp.any(
        token_routes[None, :, :] == jnp.arange(experts, dtype=jnp.int32)[:, None, None], axis=1
    )
    load = hit & live[None, :]
    seq_ids = jnp.repeat(jnp.arange(seqs, dtype=jnp.int32), block_len)
    priority = drop_order.reshape(rows) * seqs + seq_ids
    earlier = (priority[:, None] < priority[None, :]).astype(BF16)
    ahead = jnp.dot(load.astype(BF16), earlier, preferred_element_type=F32)
    slots = jnp.where(load & (ahead < cap), ahead, -1.0).astype(BF16)

    angles = local_pos.astype(F32)[:, None] * (
        ROPE_BASE ** (-2.0 * jnp.arange(HD // 2, dtype=F32) / HD)
    )
    cosine, sine = jnp.cos(angles), jnp.sin(angles)
    cosine = jnp.concatenate([cosine, cosine], axis=1)
    sine = jnp.concatenate([-sine, sine], axis=1)
    cosine_rows, sine_rows = jnp.tile(cosine, (seqs, 1)), jnp.tile(sine, (seqs, 1))

    x = layer_input.reshape(rows, width)
    grad_out = cotangent.reshape(rows, width) * live[:, None].astype(BF16)
    extra = jnp.pad(slots, ((0, 0), (0, width - rows)))
    cot_a, cot_b = grad_out[:half], jnp.concatenate([grad_out[half:], extra], axis=0)
    low_bits = list(range(len(bits_of("l"))))
    order_a, order_b = low_bits, low_bits[::-1]
    flat = lambda value: value.reshape((n_low,) + value.shape[-2:])

    def gather_low(a, b):
        a, b = open_low(a), open_low(b)
        for k in low_bits:
            a, b = gather_bit(a, order_a[k]), gather_bit(b, order_b[k])
        return flat(a), flat(b)

    cot_a, cot_b = gather_low(cot_a, cot_b)

    first_full, x, cot_a, cot_b, pair, near, far_0, output_weight = sync(
        first_full, x, cot_a, cot_b, pair, near, far_0, output_weight
    )
    small_full = first_full[:, n_q + n_kv :].T
    attn_scale = small_full[0:1].astype(F32)
    moe_scale = small_full[1:2].astype(F32)
    router_full = small_full[2 : 2 + experts]
    output_full = gather_weight(output_weight)
    far_1 = far_piece(1)
    hidden, qkv = project(x, attn_scale, first_full, cosine_rows, sine_rows)
    keyval = qkv[:, n_q:].reshape(seqs, 1, 1, block_len, n_kv)
    for bit in bits_of("h"):
        keyval = jnp.concatenate([keyval, swap(keyval, "h", bit)], axis=1)
    keyval = jnp.concatenate([keyval, swap(keyval, "c")], axis=2)
    keyval = keyval.reshape(seqs, seq_len, n_kv)
    qkv, keyval, far_0 = sync(qkv, keyval, far_0)
    far_0x = spread_high(far_0)
    posk, posq = key_pos[:, None], local_pos[None, :]
    attended, lse = attend(seq_lengths, qkv, keyval, posk, posq)

    attended, far_0x, far_1, pair = sync(attended, far_0x, far_1, pair)
    middle, tok_a, tok_b, gates = route(
        attended, output_full, x, moe_scale, router_full, hit.astype(F32)
    )
    tok_a, tok_b, near, far_1, pair, cot_a, cot_b = sync(
        tok_a, tok_b, near, far_1, pair, cot_a, cot_b
    )

    tok_a, tok_b = gather_bit(open_low(tok_a), order_a[0]), gather_bit(open_low(tok_b), order_b[0])
    far_2 = far_piece(2)
    far_1x = spread_high(far_1)
    cot_far = swap(cot_a, "c"), swap(cot_b, "c")
    whole = place((empty(n_in), empty(n_out)), 0, near, 0)
    tok_a, tok_b, far_2, far_1x, pair, whole, cot_far = sync(
        tok_a, tok_b, far_2, far_1x, pair, whole, cot_far
    )
    for k in range(1, len(low_bits)):
        tok_a, tok_b = gather_bit(tok_a, order_a[k]), gather_bit(tok_b, order_b[k])
    tok_a, tok_b = flat(tok_a), flat(tok_b)
    far_3 = far_piece(3)
    far_2x = spread_high(far_2)
    whole = place(whole, 1, far_0x, cuts[0])
    whole = place(whole, 1, far_1x, cuts[1])
    tok_a, tok_b, far_3, far_2x, whole = sync(tok_a, tok_b, far_3, far_2x, whole)
    far_3x = spread_high(far_3)
    tok_far = swap(tok_a, "c"), swap(tok_b, "c")
    whole = place(whole, 1, far_2x, cuts[2])
    far_3x, tok_far, whole = sync(far_3x, tok_far, whole)
    whole = place(whole, 1, far_3x, cuts[3])
    win, wout = joined(whole[0]), joined(whole[1])

    number = jnp.arange(2 * per_core, dtype=jnp.int32)
    side = top ^ (number // per_core)
    ids = (side * n_low + low) * local + core * per_core + number % per_core
    ids = jnp.concatenate([ids, side * per_core + number % per_core])
    step = functools.partial(experts_step, ids, cap)
    *saved, mix_n, back_an, back_bn = step(0, tok_a, tok_b, cot_a, cot_b, win, wout, ())
    *saved, mix_f, back_af, back_bf = step(1, *tok_far, *cot_far, win, wout, saved)

    back_an, back_bn, back_af, back_bf, mix_f, mix_n, saved = sync(
        back_an, back_bn, back_af, back_bf, mix_f, mix_n, saved
    )
    back_am, back_bm = swap(back_af, "c"), swap(back_bf, "c")
    picked, active, grad_both, grad_produced = (
        v.reshape(local, 2 * n_low * cap, v.shape[-1]) for v in saved
    )
    grad_wout = jnp.einsum(
        "erf,erd->efd", active, grad_produced, preferred_element_type=F32
    ).astype(BF16)
    back_am, back_bm, grad_wout, picked = sync(back_am, back_bm, grad_wout, picked)
    out_sum = scatter_expert(grad_wout, per_core)
    back_a = reduce_bit([low_axes(back_an), low_axes(back_am)], order_a[0])
    back_b = reduce_bit([low_axes(back_bn), low_axes(back_bm)], order_b[0])
    grad_win = jnp.einsum(
        "erd,erf->edf", picked, grad_both, preferred_element_type=F32
    ).astype(BF16)
    mix_m = swap(mix_f, "c")
    back_a, back_b, grad_win, mix_m = sync(back_a, back_b, grad_win, mix_m)
    in_sum = scatter_expert(grad_win, per_core)
    for k in range(1, len(low_bits)):
        back_a, back_b = reduce_bit([back_a], order_a[k]), reduce_bit([back_b], order_b[k])
    back_a, back_b = back_a.reshape(half, width), back_b.reshape(half + experts, width)

    back_a, back_b, mix_n, mix_m, out_sum = sync(back_a, back_b, mix_n, mix_m, out_sum)
    grad_middle, branch, grad_attended, router_grad, moe_gain_grad = unroute(
        back_a, back_b, gates, middle, moe_scale, router_full, grad_out, output_full
    )
    mix = reduce_bit([low_axes(p) for p in (mix_n, mix_m)], 0)
    grad_attended, branch = sync(grad_attended, branch)
    grad_output_weight = weight_core(
        jnp.dot(attended.T, branch, preferred_element_type=F32).astype(BF16)
    )
    dq, dkv = attend_back(
        seq_lengths, qkv, keyval, posk, posq, grad_attended, attended, lse, cosine, sine
    )
    dq, dkv, grad_output_weight = sync(dq, dkv, grad_output_weight)
    dkv = dkv.reshape(2, seqs, n_high, 2, block_len, KVH * HD)
    dkv = add_low(dkv[:, :, :, 0], swap(dkv[:, :, :, 1], "c"))
    grad_output_weight = weight_low(grad_output_weight)
    grad_query_weight = jnp.dot(hidden.T, dq, preferred_element_type=F32).astype(BF16)
    dkv, grad_query_weight = sync(dkv, grad_query_weight)
    for bit in reversed(bits_of("h")):
        count = dkv.shape[2] // 2
        dkv = add_low(dkv[:, :, :count], swap(dkv[:, :, count:], "h", bit))
    grad_query_weight = weight_core(grad_query_weight)
    dkv, grad_query_weight, mix = sync(dkv, grad_query_weight, mix)
    grad_query_weight = weight_bits(grad_query_weight)
    grad_input, dkv_raw, attn_gain_grad = unproject(
        x, attn_scale, grad_middle, dq, dkv.reshape(2, rows, KVH * HD), first_full,
        cosine_rows, sine_rows,
    )
    grad_keyval_weight = jnp.dot(hidden.T, dkv_raw, preferred_element_type=F32).astype(BF16)
    small_grad = jnp.concatenate([attn_gain_grad, moe_gain_grad, router_grad], axis=0)
    small_grad = jnp.pad(small_grad, ((0, HD - small_grad.shape[0]), (0, 0))).astype(BF16).T
    last = weight_core(jnp.concatenate([grad_keyval_weight, small_grad], axis=1))
    last, grad_query_weight, grad_output_weight = sync(last, grad_query_weight, grad_output_weight)
    for k in low_bits[1:]:
        mix = reduce_bit([mix], k)
    output = (middle + mix.reshape(rows, width).astype(F32)).astype(BF16)
    query_output = weight_top(jnp.concatenate([grad_query_weight, grad_output_weight], axis=2))
    last = weight_bits(last)
    last, query_output = sync(last, query_output)
    last_sum = weight_done(weight_high(weight_top(last)))
    query_output_sum = weight_done(weight_high(query_output))
    query_sum, output_sum = query_output_sum[:, :n_q], query_output_sum[:, n_q:]
    expert_out_sum, expert_in_sum = reduce_core(out_sum), reduce_core(in_sum)
    shape = (seqs, block_len, width)
    return (
        output.reshape(shape),
        grad_input.reshape(shape),
        last_sum[:, n_kv],
        query_sum,
        last_sum[:, :n_kv],
        output_sum,
        last_sum[:, n_kv + 1],
        last_sum[:, n_kv + 2 : n_kv + 2 + experts],
        expert_in_sum,
        expert_out_sum,
    )


def solution(mesh):
    ctx, shard = mesh.shape["ctx"], mesh.shape["shard"]
    cut = Mesh(mesh.devices.reshape(ctx // 2, 2, 2, shard // 2), ("h", "c", "t", "l"))
    c, s = ("h", "c"), ("t", "l")
    placed = (
        P(s, c, None),
        P(s, c, None),
        P(s),
        P(s, c, None),
        P(s, c),
        P(),
        P(s),
        P(s, None),
        P(s, None),
        P(s, None),
        P(s),
        P(s, None),
        P(s, c, None),
        P(s, c, None),
    )
    return jax.shard_map(
        per_device,
        mesh=cut,
        in_specs=placed,
        out_specs=(
            P(s, c, None),
            P(s, c, None),
            P(s),
            P(s, None),
            P(s, None),
            P(s, None),
            P(s),
            P(s, None),
            P(s, c, None),
            P(s, c, None),
        ),
        check_vma=False,
    )
```

```python
import functools

import jax
import jax.numpy as jnp
from jax import lax
from jax.experimental import pallas as pl
from jax.experimental.pallas import tpu as pltpu
from jax.sharding import Mesh
from jax.sharding import PartitionSpec as P

H = 12
KVH = 2
HD = 128
FF = 768
TOPK = 4
GROUP = H // KVH
HEADS = 2

EPSILON = 1e-06
ROPE_BASE = 10000.0
HIGHEST = lax.Precision.HIGHEST
NEG_FILL = -1e30
LOG2E = 1.4426950408889634
SCALE = HD ** (-0.5)
VMEM_LIMIT = 60 * 1024 * 1024
SMALL = pl.CostEstimate(flops=1000, bytes_accessed=1000, transcendentals=0)
F32 = jnp.float32
BF16 = jnp.bfloat16


def params(limit=VMEM_LIMIT):
    return pltpu.CompilerParams(vmem_limit_bytes=limit)


def nt(a, b, precision=None):
    return lax.dot_general(
        a, b, (((1,), (1,)), ((), ())), precision=precision, preferred_element_type=F32
    )


def tn(a, b, precision=None):
    return lax.dot_general(
        a, b, (((0,), (0,)), ((), ())), precision=precision, preferred_element_type=F32
    )


def nn(a, b, precision=None):
    return jnp.dot(a, b, precision=precision, preferred_element_type=F32)


def swap(value, axis, bit=1):
    size = lax.axis_size(axis)
    return lax.ppermute(value, axis, [(i, i ^ bit) for i in range(size)])


def bits_of(axis):
    size = lax.axis_size(axis)
    return [1 << k for k in range(size.bit_length() - 1)]


def add_low(a, b):
    return (a.astype(F32) + b.astype(F32)).astype(BF16)


def pick(value, index, axis):
    return lax.dynamic_index_in_dim(value, index, axis, keepdims=False)


def after(value, *others):
    return lax.optimization_barrier((value,) + others)[0]


def sync(*values):
    return lax.optimization_barrier(values)


def low_axes(value):
    return value.reshape((2,) * len(bits_of("l")) + value.shape[1:])


def open_low(part):
    return part.reshape((1,) * len(bits_of("l")) + part.shape)


def gather_bit(value, k):
    bits = bits_of("l")
    return jnp.concatenate([value, swap(value, "l", bits[k])], axis=len(bits) - 1 - k)


def total_of(*parts):
    return sum(p.astype(F32) for p in parts).astype(BF16)


def bit_part(value, k, index):
    axis = len(bits_of("l")) - 1 - k
    return lax.slice_in_dim(value, index, index + 1, axis=axis)


def send_bit(parts, k):
    send = total_of(*[bit_part(p, k, 1) for p in parts])
    return swap(send, "l", bits_of("l")[k])


def take_bit(parts, received, k):
    return total_of(*[bit_part(p, k, 0) for p in parts], received)


def reduce_bit(parts, k):
    return take_bit(parts, send_bit(parts, k), k)


def by_core(own, other, axis):
    return jnp.where(
        lax.axis_index("c") == 0,
        jnp.concatenate([own, other], axis=axis),
        jnp.concatenate([other, own], axis=axis),
    )


def spread_high(piece):
    pieces = [piece]
    for bit in bits_of("h"):
        pieces = pieces + [swap(p, "h", bit) for p in pieces]
    return pieces


def place_high(whole, far, pieces, first):
    high = lax.axis_index("h")
    for r, p in enumerate(pieces):
        whole = lax.dynamic_update_slice(whole, p[None, :, None], (far, 0, high ^ r, 0, first, 0))
    return whole


def joined(whole):
    return whole.reshape(whole.shape[0] * whole.shape[1], -1, whole.shape[-1])


def scatter_expert(grad, per_core):
    n_high = lax.axis_size("h")
    grad = grad.reshape(2, per_core, n_high, -1, grad.shape[-1])
    grad = jnp.swapaxes(grad, 1, 2)
    grad = grad.reshape((2 * n_high,) + grad.shape[2:])
    total = lax.psum_scatter(grad, ("t", "h"), scatter_dimension=0, tiled=True)
    return total.reshape(per_core, 2, -1, total.shape[-1])


def reduce_core(value):
    core = lax.axis_index("c")
    other = swap(pick(value, 1 - core, 1), "c")
    return by_core(pick(value, core, 1), other, 0).astype(F32)


def weight_core(grad):
    core, n_low = lax.axis_index("c"), lax.axis_size("l")
    value = grad.reshape(2, n_low, 2, -1, grad.shape[1])
    return add_low(pick(value, core, 2), swap(pick(value, 1 - core, 2), "c"))


def weight_low(value):
    value = lax.all_to_all(value, "l", split_axis=1, concat_axis=1, tiled=True)
    return jnp.sum(value.astype(F32), axis=1).astype(BF16)


def weight_bits(value):
    low = lax.axis_index("l")
    count = lax.axis_size("l")
    for bit in bits_of("l"):
        count //= 2
        value = value.reshape((2, count, 2) + value.shape[-2:])
        side = (low & bit) // bit
        value = add_low(pick(value, side, 2), swap(pick(value, 1 - side, 2), "l", bit))
    return value.reshape((2,) + value.shape[-2:])


def weight_top(value):
    top = lax.axis_index("t")
    return add_low(pick(value, top, 0), swap(pick(value, 1 - top, 0), "t"))


def weight_high(value):
    for bit in bits_of("h"):
        value = add_low(value, swap(value, "h", bit))
    return value


def weight_done(value):
    return by_core(value, swap(value, "c"), 0).astype(F32)


def norm_back(grad_normed, gain, normed, inverse):
    scaled = grad_normed * gain
    return inverse * (scaled - normed * jnp.mean(scaled * normed, axis=-1, keepdims=True))


def turn(values, cosine, sine):
    return values * cosine + pltpu.roll(values, HD // 2, 1) * sine


def project_kernel(x_ref, gain_ref, w_ref, cos_ref, sin_ref, hidden_ref, out_ref):
    step = pl.program_id(0)

    @pl.when(step == 0)
    def _():
        x = x_ref[...].astype(F32)
        inverse = lax.rsqrt(jnp.mean(x * x, axis=-1, keepdims=True) + EPSILON)
        hidden_ref[...] = ((x * inverse) * gain_ref[...]).astype(BF16)

    raw = nn(hidden_ref[...], w_ref[...])
    per_step = raw.shape[1] // HD
    for k in range(per_step):
        head = raw[:, k * HD : (k + 1) * HD]
        turned = turn(head, cos_ref[...], sin_ref[...])
        is_value = step * per_step + k >= H + KVH
        out_ref[:, k * HD : (k + 1) * HD] = jnp.where(is_value, head, turned).astype(BF16)


def project(x, gain, weight, cosine, sine):
    rows, width = x.shape
    columns = (H + 2 * KVH) * HD
    block = 512
    return pl.pallas_call(
        project_kernel,
        grid=(columns // block,),
        in_specs=[
            pl.BlockSpec((rows, width), lambda i: (0, 0)),
            pl.BlockSpec((1, width), lambda i: (0, 0)),
            pl.BlockSpec((width, block), lambda i: (0, i)),
            pl.BlockSpec((rows, HD), lambda i: (0, 0)),
            pl.BlockSpec((rows, HD), lambda i: (0, 0)),
        ],
        out_specs=[
            pl.BlockSpec((rows, width), lambda i: (0, 0)),
            pl.BlockSpec((rows, block), lambda i: (0, i)),
        ],
        out_shape=[
            jax.ShapeDtypeStruct((rows, width), BF16),
            jax.ShapeDtypeStruct((rows, columns), BF16),
        ],
        compiler_params=params(),
        cost_estimate=SMALL,
        name="project",
    )(x, gain, weight, cosine, sine)


def set_bias(len_ref, posk_ref, posq_ref, bias):
    seq = pl.program_id(0)

    @pl.when((pl.program_id(1) == 0) & (pl.program_id(2) == 0))
    def _():
        posk = posk_ref[...]
        allowed = (posk <= posq_ref[...]) & (posk < len_ref[seq])
        bias[...] = jnp.where(allowed, 0.0, NEG_FILL)


def attend_kernel(len_ref, q_ref, k_ref, v_ref, posk_ref, posq_ref, out_ref, lse_ref, bias, turned):
    set_bias(len_ref, posk_ref, posq_ref, bias)

    @pl.when(pl.program_id(2) == 0)
    def _():
        turned[...] = v_ref[0].T

    for k in range(HEADS):
        part = slice(k * HD, (k + 1) * HD)
        scores = nt(k_ref[0], q_ref[:, part]) * (SCALE * LOG2E) + bias[...]
        top = jnp.max(scores, axis=0, keepdims=True)
        weights = jnp.exp2(scores - top)
        total = jnp.sum(weights, axis=0, keepdims=True)
        mixed = nn(turned[...], weights.astype(BF16)) * (1.0 / total)
        out_ref[:, part] = mixed.T.astype(BF16)
        lse_ref[0, k] = top + jnp.log2(total)


def attend(lengths, qkv, keyval, posk, posq):
    seqs, keys, _ = keyval.shape
    rows = qkv.shape[0] // seqs
    return pl.pallas_call(
        attend_kernel,
        grid_spec=pltpu.PrefetchScalarGridSpec(
            num_scalar_prefetch=1,
            grid=(seqs, KVH, GROUP // HEADS),
            in_specs=[
                pl.BlockSpec((rows, HEADS * HD), lambda s, g, h, n: (s, g * (GROUP // HEADS) + h)),
                pl.BlockSpec((1, keys, HD), lambda s, g, h, n: (s, 0, g)),
                pl.BlockSpec((1, keys, HD), lambda s, g, h, n: (s, 0, KVH + g)),
                pl.BlockSpec((keys, 1), lambda s, g, h, n: (0, 0)),
                pl.BlockSpec((1, rows), lambda s, g, h, n: (0, 0)),
            ],
            out_specs=[
                pl.BlockSpec((rows, HEADS * HD), lambda s, g, h, n: (s, g * (GROUP // HEADS) + h)),
                pl.BlockSpec((1, HEADS, 1, rows), lambda s, g, h, n: (s, g * (GROUP // HEADS) + h, 0, 0)),
            ],
            scratch_shapes=[pltpu.VMEM((keys, rows), F32), pltpu.VMEM((HD, keys), BF16)],
        ),
        out_shape=[
            jax.ShapeDtypeStruct((seqs * rows, H * HD), BF16),
            jax.ShapeDtypeStruct((seqs, H, 1, rows), F32),
        ],
        compiler_params=params(),
        cost_estimate=SMALL,
        name="attend",
    )(lengths, qkv, keyval, keyval, posk, posq)


def attend_back_kernel(
    len_ref, q_ref, k_ref, v_ref, posk_ref, posq_ref, grad_ref, out_ref, lse_ref, cos_ref, sin_ref,
    dq_ref, dkv_ref, bias, turned, dk, dv,
):
    set_bias(len_ref, posk_ref, posq_ref, bias)
    head = pl.program_id(2)

    @pl.when(head == 0)
    def _():
        turned[...] = k_ref[0].T
        dk[...] = jnp.zeros_like(dk)
        dv[...] = jnp.zeros_like(dv)

    for k in range(HEADS):
        part = slice(k * HD, (k + 1) * HD)
        q, grad = q_ref[:, part], grad_ref[:, part]
        scores = nt(k_ref[0], q) * (SCALE * LOG2E) + bias[...]
        probs = jnp.exp2(scores - lse_ref[0, k])
        grad_probs = nt(v_ref[0], grad)
        product = grad.astype(F32) * out_ref[:, part].astype(F32)
        delta = jnp.sum(product.T, axis=0, keepdims=True)
        grad_scores = (probs * (grad_probs - delta)).astype(BF16)
        dv[...] += nn(probs.astype(BF16), grad)
        dk[...] += nn(grad_scores, q)
        dq = nn(turned[...], grad_scores).T * SCALE
        dq_ref[:, part] = turn(dq, cos_ref[...], -sin_ref[...]).astype(BF16)

    @pl.when(head == GROUP // HEADS - 1)
    def _():
        dkv_ref[0, 0] = (dk[...] * SCALE).astype(BF16)
        dkv_ref[1, 0] = dv[...].astype(BF16)


def attend_back(lengths, qkv, keyval, posk, posq, grad, attended, lse, cosine, sine):
    seqs, keys, _ = keyval.shape
    rows = qkv.shape[0] // seqs
    heads = pl.BlockSpec((rows, HEADS * HD), lambda s, g, h, n: (s, g * (GROUP // HEADS) + h))
    table = pl.BlockSpec((rows, HD), lambda s, g, h, n: (0, 0))
    return pl.pallas_call(
        attend_back_kernel,
        grid_spec=pltpu.PrefetchScalarGridSpec(
            num_scalar_prefetch=1,
            grid=(seqs, KVH, GROUP // HEADS),
            in_specs=[
                heads,
                pl.BlockSpec((1, keys, HD), lambda s, g, h, n: (s, 0, g)),
                pl.BlockSpec((1, keys, HD), lambda s, g, h, n: (s, 0, KVH + g)),
                pl.BlockSpec((keys, 1), lambda s, g, h, n: (0, 0)),
                pl.BlockSpec((1, rows), lambda s, g, h, n: (0, 0)),
                heads,
                heads,
                pl.BlockSpec((1, HEADS, 1, rows), lambda s, g, h, n: (s, g * (GROUP // HEADS) + h, 0, 0)),
                table,
                table,
            ],
            out_specs=[
                heads,
                pl.BlockSpec((2, 1, keys, HD), lambda s, g, h, n: (0, s, 0, g)),
            ],
            scratch_shapes=[
                pltpu.VMEM((keys, rows), F32),
                pltpu.VMEM((HD, keys), BF16),
                pltpu.VMEM((keys, HD), F32),
                pltpu.VMEM((keys, HD), F32),
            ],
        ),
        out_shape=[
            jax.ShapeDtypeStruct((seqs * rows, H * HD), BF16),
            jax.ShapeDtypeStruct((2, seqs, keys, KVH * HD), BF16),
        ],
        compiler_params=params(),
        cost_estimate=SMALL,
        name="attend_back",
    )(lengths, qkv, keyval, keyval, posk, posq, grad, attended, lse, cosine, sine)


def route_kernel(
    att_ref, w_ref, x_ref, gain_ref, router_ref, hit_ref, middle_ref, first_ref, second_ref, gates_ref
):
    rows = x_ref.shape[0]
    experts = hit_ref.shape[0]
    middle = x_ref[...].astype(F32) + nn(att_ref[...], w_ref[...])
    middle_ref[...] = middle
    inverse = lax.rsqrt(jnp.mean(middle * middle, axis=-1, keepdims=True) + EPSILON)
    tokens = ((middle * inverse) * gain_ref[...]).astype(BF16)
    first_ref[...] = tokens[: rows // 2]
    second_ref[: rows // 2] = tokens[rows // 2 :]
    hit = hit_ref[...] > 0
    logits = jnp.where(hit, nt(router_ref[...], tokens), NEG_FILL)
    raised = jnp.where(hit, jnp.exp(logits - jnp.max(logits, axis=0, keepdims=True)), 0.0)
    gates = raised / jnp.sum(raised, axis=0, keepdims=True)
    gates_ref[...] = gates
    coarse = gates.astype(BF16)
    fine = (gates - coarse.astype(F32)).astype(BF16)
    second_ref[rows // 2 :, :rows] = coarse
    second_ref[rows // 2 :, rows : 2 * rows] = fine
    second_ref[rows // 2 :, 2 * rows :] = jnp.zeros(
        (experts, second_ref.shape[1] - 2 * rows), BF16
    )


def route(attended, weight, x, gain, router, hit):
    rows, width = x.shape
    experts = hit.shape[0]
    return pl.pallas_call(
        route_kernel,
        out_shape=[
            jax.ShapeDtypeStruct((rows, width), F32),
            jax.ShapeDtypeStruct((rows // 2, width), BF16),
            jax.ShapeDtypeStruct((rows // 2 + experts, width), BF16),
            jax.ShapeDtypeStruct((experts, rows), F32),
        ],
        compiler_params=params(),
        cost_estimate=SMALL,
        name="route",
    )(attended, weight, x, gain, router, hit)


def expert_kernel(
    cap, ids_ref, tok_a, tok_b, cot_a, cot_b, win_ref, wout_ref, *refs
):
    x_ref, active_ref, both_ref, grad_ref, mix_ref, back_a, back_b = refs[-7:]
    number = pl.program_id(1)
    mine = ids_ref[number]
    half = tok_a.shape[1]
    rows = 2 * half
    experts = tok_b.shape[1] - half
    width = tok_a.shape[2]
    row_is_mine = lax.broadcasted_iota(jnp.int32, (experts, 1), 0) == mine

    def own_row(values):
        return jnp.sum(jnp.where(row_is_mine, values.astype(F32), 0.0), axis=0, keepdims=True)

    hits, spreads, gates, picked, grads = [], [], [], [], []
    for g in range(2):
        slot = own_row(cot_b[g, half:, :rows]).astype(jnp.int32)
        gate_row = own_row(
            tok_b[g, half:, :rows].astype(F32) + tok_b[g, half:, rows : 2 * rows].astype(F32)
        )
        hit = lax.broadcasted_iota(jnp.int32, (cap, rows), 0) == slot
        spread = jnp.where(hit, 1.0, 0.0).astype(BF16)
        hits.append(hit)
        spreads.append(spread)
        gates.append(jnp.sum(jnp.where(hit, gate_row, 0.0), axis=1, keepdims=True))
        picked.append(nn(spread[:, :half], tok_a[g]) + nn(spread[:, half:], tok_b[g, :half]))
        grads.append(nn(spread[:, :half], cot_a[g]) + nn(spread[:, half:], cot_b[g, :half]))
    tokens = jnp.concatenate(picked, axis=0).astype(BF16)
    grad_out = jnp.concatenate(grads, axis=0)
    gate = jnp.concatenate(gates, axis=0)
    x_ref[0, 0] = tokens.reshape(2, cap, width)
    both = nn(tokens, win_ref[0])
    gate_part, up_part = both[:, :FF], both[:, FF:]
    sigmoid = 1.0 / (1.0 + jnp.exp(-gate_part))
    silu = gate_part * sigmoid
    active = (silu * up_part).astype(BF16)
    active_ref[0, 0] = active.reshape(2, cap, FF)
    produced = nn(active, wout_ref[0]).astype(BF16).astype(F32)
    grad_gate = jnp.sum(produced * grad_out, axis=1, keepdims=True)
    weighed = (produced * gate).astype(BF16)
    grad_produced = (grad_out * gate).astype(BF16)
    grad_ref[0, 0] = grad_produced.reshape(2, cap, width)
    grad_active = nt(grad_produced, wout_ref[0])
    grad_both = jnp.concatenate(
        [
            grad_active * up_part * sigmoid * (1.0 + gate_part * (1.0 - sigmoid)),
            grad_active * silu,
        ],
        axis=1,
    ).astype(BF16)
    both_ref[0, 0] = grad_both.reshape(2, cap, 2 * FF)
    grad_rows = nt(grad_both, win_ref[0]).astype(BF16)

    @pl.when(number == 0)
    def _():
        mix_ref[...] = jnp.zeros_like(mix_ref)
        back_a[...] = jnp.zeros_like(back_a)
        back_b[...] = jnp.zeros_like(back_b)

    for g in range(2):
        part = slice(g * cap, (g + 1) * cap)
        sums = tn(spreads[g], jnp.concatenate([weighed[part], grad_rows[part]], axis=1))
        mix_ref[g] = (mix_ref[g].astype(F32) + sums[:, :width]).astype(BF16)
        back = sums[:, width:]
        back_a[g] = (back_a[g].astype(F32) + back[:half]).astype(BF16)
        back_b[g, :half] = (back_b[g, :half].astype(F32) + back[half:]).astype(BF16)
        dense = jnp.sum(jnp.where(hits[g], grad_gate[part], 0.0), axis=0, keepdims=True)
        coarse = dense.astype(BF16).astype(F32)
        fine = dense - coarse
        back_b[g, half:, :rows] += jnp.where(row_is_mine, coarse, 0.0).astype(BF16)
        back_b[g, half:, rows : 2 * rows] += jnp.where(row_is_mine, fine, 0.0).astype(BF16)


def experts_step(ids, cap, side, tok_a, tok_b, cot_a, cot_b, win, wout, earlier):
    n_low, half, width = tok_a.shape
    experts = tok_b.shape[1] - half
    local = win.shape[0]
    tokens = lambda n: pl.BlockSpec((2, n, width), lambda i, j, ids: (i, 0, 0))
    rows = lambda n: pl.BlockSpec(
        (1, 1, 2, cap, n), lambda i, j, ids: (ids[local + j], side, i, 0, 0)
    )
    rows_shape = lambda n: jax.ShapeDtypeStruct((local, 2, n_low, cap, n), BF16)
    weights = lambda w: pl.BlockSpec((1,) + w.shape[1:], lambda i, j, ids: (j, 0, 0))
    earlier = tuple(earlier)
    n_rows = local * n_low * cap
    return pl.pallas_call(
        functools.partial(expert_kernel, cap),
        grid_spec=pltpu.PrefetchScalarGridSpec(
            num_scalar_prefetch=1,
            grid=(n_low // 2, local),
            in_specs=[
                tokens(half),
                tokens(half + experts),
                tokens(half),
                tokens(half + experts),
                weights(win),
                weights(wout),
            ]
            + [pl.BlockSpec(memory_space=pl.ANY)] * len(earlier),
            out_specs=[
                rows(width),
                rows(FF),
                rows(2 * FF),
                rows(width),
                tokens(2 * half),
                tokens(half),
                tokens(half + experts),
            ],
        ),
        out_shape=[
            rows_shape(width),
            rows_shape(FF),
            rows_shape(2 * FF),
            rows_shape(width),
            jax.ShapeDtypeStruct((n_low, 2 * half, width), BF16),
            jax.ShapeDtypeStruct((n_low, half, width), BF16),
            jax.ShapeDtypeStruct((n_low, half + experts, width), BF16),
        ],
        input_output_aliases={7 + k: k for k in range(len(earlier))},
        compiler_params=params(),
        cost_estimate=SMALL,
        name="experts",
    )(ids, tok_a, tok_b, cot_a, cot_b, win, wout, *earlier)


def unroute_kernel(
    first_ref, second_ref, gates_ref, middle_ref, gain_ref, router_ref, cot_ref, w_ref,
    grad_ref, branch_ref, att_ref, router_grad_ref, gain_grad_ref,
):
    rows = middle_ref.shape[0]
    half = rows // 2
    gates = gates_ref[...]
    grad_gate = second_ref[half:, :rows].astype(F32) + second_ref[half:, rows : 2 * rows].astype(F32)
    grad_logits = gates * (grad_gate - jnp.sum(gates * grad_gate, axis=0, keepdims=True))
    middle = middle_ref[...]
    inverse = lax.rsqrt(jnp.mean(middle * middle, axis=-1, keepdims=True) + EPSILON)
    normed = middle * inverse
    tokens = (normed * gain_ref[...]).astype(BF16)
    coarse = grad_logits.astype(BF16)
    fine = (grad_logits - coarse.astype(F32)).astype(BF16)
    router_grad_ref[...] = nn(coarse, tokens) + nn(fine, tokens)
    grad_tokens = jnp.concatenate([first_ref[...], second_ref[:half]], axis=0).astype(F32)
    grad_tokens = grad_tokens + tn(coarse, router_ref[...]) + tn(fine, router_ref[...])
    gain_grad_ref[...] = jnp.sum(grad_tokens * normed, axis=0, keepdims=True)
    grad_middle = cot_ref[...].astype(F32) + norm_back(grad_tokens, gain_ref[...], normed, inverse)
    grad_ref[...] = grad_middle
    branch = grad_middle.astype(BF16)
    branch_ref[...] = branch
    att_ref[...] = nt(branch, w_ref[...]).astype(BF16)


def unroute(first, second, gates, middle, gain, router, cotangent, weight):
    rows, width = middle.shape
    experts = gates.shape[0]
    return pl.pallas_call(
        unroute_kernel,
        out_shape=[
            jax.ShapeDtypeStruct((rows, width), F32),
            jax.ShapeDtypeStruct((rows, width), BF16),
            jax.ShapeDtypeStruct((rows, width), BF16),
            jax.ShapeDtypeStruct((experts, width), F32),
            jax.ShapeDtypeStruct((1, width), F32),
        ],
        compiler_params=params(),
        cost_estimate=SMALL,
        name="unroute",
    )(first, second, gates, middle, gain, router, cotangent, weight)


def unproject_kernel(
    x_ref, gain_ref, grad_ref, dq_ref, dkv_ref, w_ref, cos_ref, sin_ref, out_ref, dkv_raw_ref, gain_grad_ref
):
    rows, width = x_ref.shape
    for k in range(KVH):
        part = slice(k * HD, (k + 1) * HD)
        dkv_raw_ref[:, part] = turn(
            dkv_ref[0, :, part].astype(F32), cos_ref[...], -sin_ref[...]
        ).astype(BF16)
    dkv_raw_ref[:, KVH * HD :] = dkv_ref[1]
    n_query = dq_ref.shape[1]
    grad_hidden = nt(dq_ref[...], w_ref[:, :n_query]) + nt(
        dkv_raw_ref[...], w_ref[:, n_query : n_query + 2 * KVH * HD]
    )
    x = x_ref[...].astype(F32)
    inverse = lax.rsqrt(jnp.mean(x * x, axis=-1, keepdims=True) + EPSILON)
    normed = x * inverse
    gain_grad_ref[...] = jnp.sum(grad_hidden * normed, axis=0, keepdims=True)
    out_ref[...] = (
        grad_ref[...] + norm_back(grad_hidden, gain_ref[...], normed, inverse)
    ).astype(BF16)


def unproject(x, gain, grad_middle, dq, dkv, weight, cosine, sine):
    rows, width = x.shape
    return pl.pallas_call(
        unproject_kernel,
        out_shape=[
            jax.ShapeDtypeStruct((rows, width), BF16),
            jax.ShapeDtypeStruct((rows, 2 * KVH * HD), BF16),
            jax.ShapeDtypeStruct((1, width), F32),
        ],
        compiler_params=params(),
        cost_estimate=SMALL,
        name="unproject",
    )(x, gain, grad_middle, dq, dkv, weight, cosine, sine)


def place_blocks(block_order, storage, sub_len):
    blocks = storage // sub_len
    matches = blocks[:, None] == jnp.arange(block_order.shape[0], dtype=jnp.int32)[None, :]
    return (
        jnp.sum(jnp.where(matches, block_order[None, :], 0), axis=1) * sub_len + storage % sub_len
    )


def per_device(
    layer_input,
    cotangent,
    seq_lengths,
    routes,
    drop_order,
    block_order,
    attn_gain,
    query_weight,
    keyval_weight,
    output_weight,
    moe_gain,
    router_weight,
    expert_in,
    expert_out,
):
    seqs, block_len, width = layer_input.shape
    core, high = lax.axis_index("c"), lax.axis_index("h")
    top, low = lax.axis_index("t"), lax.axis_index("l")
    n_high, n_low = lax.axis_size("h"), lax.axis_size("l")
    ctx_size, shard_size = 2 * n_high, 2 * n_low
    rows = seqs * block_len
    seq_len = block_len * ctx_size
    local = expert_in.shape[0]
    experts = local * shard_size
    cap = (5 * rows * TOPK + 4 * experts - 1) // (4 * experts)
    half = rows // 2

    n_in, n_out = expert_in.shape[1], expert_out.shape[1]
    per_core = local // 2
    packed = jnp.concatenate([expert_in, expert_out], axis=1)
    own = lax.dynamic_slice_in_dim(packed, core * per_core, per_core, 0)
    away = lax.dynamic_slice_in_dim(packed, (1 - core) * per_core, per_core, 0)
    other = swap(away, "c")
    pair = by_core(own[:, None], other[:, None], 1)
    near = spread_high(pair)
    unit = (n_in + n_out) // 36
    cuts = [k * unit for k in (0, 14, 20, 29)] + [n_in + n_out]
    far_piece = lambda k: swap(pair[:, :, cuts[k] : cuts[k + 1]], "t")
    empty = lambda n: jnp.zeros((2, per_core, n_high, 2, n, width), BF16)

    def place(whole, far, pieces, first):
        count = pieces[0].shape[2]
        split = min(max(n_in - first, 0), count)
        if split > 0:
            whole = (place_high(whole[0], far, [p[:, :, :split] for p in pieces], first), whole[1])
        if split < count:
            rest = [p[:, :, split:] for p in pieces]
            whole = (whole[0], place_high(whole[1], far, rest, first + split - n_in))
        return whole

    far_0 = far_piece(0)

    small = jnp.concatenate([attn_gain[:, None], moe_gain[:, None], router_weight], axis=1)
    small = jnp.pad(small, ((0, 0), (0, HD - small.shape[1])))
    n_q, n_kv = query_weight.shape[1], keyval_weight.shape[1]

    def gather_weight(part):
        own = pick(part.reshape(2, -1, part.shape[1]), core, 0)
        return lax.all_gather(own, ("t", "l", "c"), axis=0, tiled=True)

    first_full = gather_weight(
        after(jnp.concatenate([query_weight, keyval_weight, small], axis=1), other)
    )

    sub_len = seq_len // block_order.shape[0]
    inner = jnp.arange(block_len, dtype=jnp.int32)
    local_pos = place_blocks(block_order, (high * 2 + core) * block_len + inner, sub_len)
    relative = jnp.arange(ctx_size, dtype=jnp.int32)
    key_ctx = ((relative // 2) ^ high) * 2 + ((relative % 2) ^ core)
    key_pos = place_blocks(
        block_order, (key_ctx[:, None] * block_len + inner[None, :]).reshape(-1), sub_len
    )
    live = (local_pos[None, :] < seq_lengths[:, None]).reshape(rows)
    token_routes = routes.reshape(rows, TOPK).T
    hit = jnp.any(
        token_routes[None, :, :] == jnp.arange(experts, dtype=jnp.int32)[:, None, None], axis=1
    )
    load = hit & live[None, :]
    seq_ids = jnp.repeat(jnp.arange(seqs, dtype=jnp.int32), block_len)
    priority = drop_order.reshape(rows) * seqs + seq_ids
    earlier = (priority[:, None] < priority[None, :]).astype(BF16)
    ahead = jnp.dot(load.astype(BF16), earlier, preferred_element_type=F32)
    slots = jnp.where(load & (ahead < cap), ahead, -1.0).astype(BF16)

    angles = local_pos.astype(F32)[:, None] * (
        ROPE_BASE ** (-2.0 * jnp.arange(HD // 2, dtype=F32) / HD)
    )
    cosine, sine = jnp.cos(angles), jnp.sin(angles)
    cosine = jnp.concatenate([cosine, cosine], axis=1)
    sine = jnp.concatenate([-sine, sine], axis=1)
    cosine_rows, sine_rows = jnp.tile(cosine, (seqs, 1)), jnp.tile(sine, (seqs, 1))

    x = layer_input.reshape(rows, width)
    grad_out = cotangent.reshape(rows, width) * live[:, None].astype(BF16)
    extra = jnp.pad(slots, ((0, 0), (0, width - rows)))
    cot_a, cot_b = grad_out[:half], jnp.concatenate([grad_out[half:], extra], axis=0)
    low_bits = list(range(len(bits_of("l"))))
    order_a, order_b = low_bits, low_bits[::-1]
    flat = lambda value: value.reshape((n_low,) + value.shape[-2:])

    def gather_low(a, b):
        a, b = open_low(a), open_low(b)
        for k in low_bits:
            a, b = gather_bit(a, order_a[k]), gather_bit(b, order_b[k])
        return flat(a), flat(b)

    cot_a, cot_b = gather_low(cot_a, cot_b)

    first_full, x, cot_a, cot_b, pair, near, far_0, output_weight = sync(
        first_full, x, cot_a, cot_b, pair, near, far_0, output_weight
    )
    small_full = first_full[:, n_q + n_kv :].T
    attn_scale = small_full[0:1].astype(F32)
    moe_scale = small_full[1:2].astype(F32)
    router_full = small_full[2 : 2 + experts]
    output_full = gather_weight(output_weight)
    far_1 = far_piece(1)
    hidden, qkv = project(x, attn_scale, first_full, cosine_rows, sine_rows)
    keyval = qkv[:, n_q:].reshape(seqs, 1, 1, block_len, n_kv)
    for bit in bits_of("h"):
        keyval = jnp.concatenate([keyval, swap(keyval, "h", bit)], axis=1)
    keyval = jnp.concatenate([keyval, swap(keyval, "c")], axis=2)
    keyval = keyval.reshape(seqs, seq_len, n_kv)
    qkv, keyval, far_0 = sync(qkv, keyval, far_0)
    far_0x = spread_high(far_0)
    posk, posq = key_pos[:, None], local_pos[None, :]
    attended, lse = attend(seq_lengths, qkv, keyval, posk, posq)

    attended, far_0x, far_1, pair = sync(attended, far_0x, far_1, pair)
    middle, tok_a, tok_b, gates = route(
        attended, output_full, x, moe_scale, router_full, hit.astype(F32)
    )
    tok_a, tok_b, near, far_1, pair, cot_a, cot_b = sync(
        tok_a, tok_b, near, far_1, pair, cot_a, cot_b
    )

    tok_a, tok_b = gather_bit(open_low(tok_a), order_a[0]), gather_bit(open_low(tok_b), order_b[0])
    far_2 = far_piece(2)
    far_1x = spread_high(far_1)
    cot_far = swap(cot_a, "c"), swap(cot_b, "c")
    whole = place((empty(n_in), empty(n_out)), 0, near, 0)
    tok_a, tok_b, far_2, far_1x, pair, whole, cot_far = sync(
        tok_a, tok_b, far_2, far_1x, pair, whole, cot_far
    )
    for k in range(1, len(low_bits)):
        tok_a, tok_b = gather_bit(tok_a, order_a[k]), gather_bit(tok_b, order_b[k])
    tok_a, tok_b = flat(tok_a), flat(tok_b)
    far_3 = far_piece(3)
    far_2x = spread_high(far_2)
    whole = place(whole, 1, far_0x, cuts[0])
    whole = place(whole, 1, far_1x, cuts[1])
    tok_a, tok_b, far_3, far_2x, whole = sync(tok_a, tok_b, far_3, far_2x, whole)
    far_3x = spread_high(far_3)
    tok_far = swap(tok_a, "c"), swap(tok_b, "c")
    whole = place(whole, 1, far_2x, cuts[2])
    far_3x, tok_far, whole = sync(far_3x, tok_far, whole)
    whole = place(whole, 1, far_3x, cuts[3])
    win, wout = joined(whole[0]), joined(whole[1])

    number = jnp.arange(2 * per_core, dtype=jnp.int32)
    side = top ^ (number // per_core)
    ids = (side * n_low + low) * local + core * per_core + number % per_core
    ids = jnp.concatenate([ids, side * per_core + number % per_core])
    step = functools.partial(experts_step, ids, cap)
    *saved, mix_f, back_af, back_bf = step(1, *tok_far, *cot_far, win, wout, ())
    saved, mix_f, back_af, back_bf = sync(saved, mix_f, back_af, back_bf)
    back_am, back_bm, mix_m = swap(back_af, "c"), swap(back_bf, "c"), swap(mix_f, "c")
    *saved, mix_n, back_an, back_bn = step(0, tok_a, tok_b, cot_a, cot_b, win, wout, saved)

    back_an, back_bn, back_am, back_bm, mix_m, mix_n, saved = sync(
        back_an, back_bn, back_am, back_bm, mix_m, mix_n, saved
    )
    back_a = reduce_bit([low_axes(back_an), low_axes(back_am)], order_a[0])
    back_b = reduce_bit([low_axes(back_bn), low_axes(back_bm)], order_b[0])
    picked, active, grad_both, grad_produced = (
        v.reshape(local, 2 * n_low * cap, v.shape[-1]) for v in saved
    )
    grad_wout = jnp.einsum(
        "erf,erd->efd", active, grad_produced, preferred_element_type=F32
    ).astype(BF16)
    out_sum = scatter_expert(grad_wout, per_core)
    grad_win = jnp.einsum(
        "erd,erf->edf", picked, after(grad_both, grad_wout), preferred_element_type=F32
    ).astype(BF16)
    back_a, back_b, grad_win, mix_n, mix_m = sync(back_a, back_b, grad_win, mix_n, mix_m)
    in_sum = scatter_expert(grad_win, per_core)
    mix = send_bit([low_axes(p) for p in (mix_n, mix_m)], 0)
    for k in range(1, len(low_bits)):
        back_a, back_b = reduce_bit([back_a], order_a[k]), reduce_bit([back_b], order_b[k])
    back_a, back_b = back_a.reshape(half, width), back_b.reshape(half + experts, width)

    back_a, back_b, out_sum = sync(back_a, back_b, out_sum)
    grad_middle, branch, grad_attended, router_grad, moe_gain_grad = unroute(
        back_a, back_b, gates, middle, moe_scale, router_full, grad_out, output_full
    )
    grad_attended, branch = sync(grad_attended, branch)
    grad_output_weight = weight_core(
        jnp.dot(attended.T, branch, preferred_element_type=F32).astype(BF16)
    )
    dq, dkv = attend_back(
        seq_lengths, qkv, keyval, posk, posq, grad_attended, attended, lse, cosine, sine
    )
    dq, dkv, grad_output_weight, mix, mix_n = sync(dq, dkv, grad_output_weight, mix, mix_n)
    mix = take_bit([low_axes(p) for p in (mix_n, mix_m)], mix, 0)
    dkv = dkv.reshape(2, seqs, n_high, 2, block_len, KVH * HD)
    dkv = add_low(dkv[:, :, :, 0], swap(dkv[:, :, :, 1], "c"))
    grad_output_weight = weight_low(grad_output_weight)
    grad_query_weight = jnp.dot(hidden.T, dq, preferred_element_type=F32).astype(BF16)
    dkv, grad_query_weight = sync(dkv, grad_query_weight)
    for bit in reversed(bits_of("h")):
        count = dkv.shape[2] // 2
        dkv = add_low(dkv[:, :, :count], swap(dkv[:, :, count:], "h", bit))
    grad_query_weight = weight_core(grad_query_weight)
    dkv, grad_query_weight, mix = sync(dkv, grad_query_weight, mix)
    grad_query_weight = weight_bits(grad_query_weight)
    grad_input, dkv_raw, attn_gain_grad = unproject(
        x, attn_scale, grad_middle, dq, dkv.reshape(2, rows, KVH * HD), first_full,
        cosine_rows, sine_rows,
    )
    grad_keyval_weight = jnp.dot(hidden.T, dkv_raw, preferred_element_type=F32).astype(BF16)
    small_grad = jnp.concatenate([attn_gain_grad, moe_gain_grad, router_grad], axis=0)
    small_grad = jnp.pad(small_grad, ((0, HD - small_grad.shape[0]), (0, 0))).astype(BF16).T
    last = weight_core(jnp.concatenate([grad_keyval_weight, small_grad], axis=1))
    last, grad_query_weight, grad_output_weight, mix = sync(
        last, grad_query_weight, grad_output_weight, mix
    )
    for k in low_bits[1:]:
        mix = reduce_bit([mix], k)
    query_output = weight_top(jnp.concatenate([grad_query_weight, grad_output_weight], axis=2))
    last = weight_bits(last)
    last, query_output, mix = sync(last, query_output, mix)
    last_sum = weight_done(weight_high(weight_top(last)))
    query_output_sum = weight_done(weight_high(query_output))
    output = (middle + mix.reshape(rows, width).astype(F32)).astype(BF16)
    query_sum, output_sum = query_output_sum[:, :n_q], query_output_sum[:, n_q:]
    expert_out_sum, expert_in_sum = reduce_core(out_sum), reduce_core(in_sum)
    shape = (seqs, block_len, width)
    return (
        output.reshape(shape),
        grad_input.reshape(shape),
        last_sum[:, n_kv],
        query_sum,
        last_sum[:, :n_kv],
        output_sum,
        last_sum[:, n_kv + 1],
        last_sum[:, n_kv + 2 : n_kv + 2 + experts],
        expert_in_sum,
        expert_out_sum,
    )


def solution(mesh):
    ctx, shard = mesh.shape["ctx"], mesh.shape["shard"]
    cut = Mesh(mesh.devices.reshape(ctx // 2, 2, 2, shard // 2), ("h", "c", "t", "l"))
    c, s = ("h", "c"), ("t", "l")
    placed = (
        P(s, c, None),
        P(s, c, None),
        P(s),
        P(s, c, None),
        P(s, c),
        P(),
        P(s),
        P(s, None),
        P(s, None),
        P(s, None),
        P(s),
        P(s, None),
        P(s, c, None),
        P(s, c, None),
    )
    return jax.shard_map(
        per_device,
        mesh=cut,
        in_specs=placed,
        out_specs=(
            P(s, c, None),
            P(s, c, None),
            P(s),
            P(s, None),
            P(s, None),
            P(s, None),
            P(s),
            P(s, None),
            P(s, c, None),
            P(s, c, None),
        ),
        check_vma=False,
    )
```
